256 devices in a mesh: ens: 8 (over x, y_lo), lat: 32 (over z, y_hi, core).
Axes of the slice: x: 4, y: 4 (y_hi: 2, y_lo: 2; y = y_hi * 2 + y_lo), z: 8, core: 2. Of those that a mesh axis runs over, the one named last changes fastest.
Arguments:
- features: bfloat16 [8, 128, 1440, 256], P('ens', 'lat'), may hold values from -6 to 6
- previous: bfloat16 [8, 72, 128, 1440], P('ens', None, 'lat'), may hold values from -6 to 6
- target: bfloat16 [72, 128, 1440], P(None, 'lat'), may hold values from -8 to 8
- weight: bfloat16 [256, 72], replicated, may hold values from -0.375 to 0.375
- var_weight: float32 [72], replicated, may hold values from 0.2 to 2
Outputs:
- spectral_grad: bfloat16 [8, 352, 352, 2, 256], P('ens', 'lat')
- weight_grad: float32 [256, 72], replicated
The draws below stay inside these ranges and needn't reach their ends.
All inputs are finite; a program needn't handle non-finite values.
Results may differ from the reference program's by a relative error of at most 0.005.
Values may be sent and summed in bfloat16 or wider, within the bound.
A program may use at most 128 MiB of HBM per device.

```python
import math
import jax
import jax.numpy as jnp
from jax import lax

MEMBER_COUNT = 8
FULL_LAT = 721
NLAT = 128
BAND_START = 296
NLON = 1440
C = 256
VARS = 72
ORDERS = 352
DEGREES = 352


def shard_levels(own_key, dims, cuts, smallest, high):
    def one(position, shards_of):
        heights = jax.random.uniform(jax.random.fold_in(jax.random.fold_in(own_key, 6), position), (shards_of,), jnp.float32, smallest / len(cuts), high / len(cuts))
        return jnp.repeat(jnp.exp(heights), dims[position] // shards_of).reshape((-1,) + (1,) * (len(dims) - position - 1))

    gain = one(*cuts[0])
    for cut in cuts[1:]:
        gain = gain * one(*cut)
    return gain


def normal_values(own_key, extent, scale, most, split=(), kind=jnp.bfloat16):
    values = jax.random.normal(own_key, extent, jnp.float32) * scale
    if len(split) > 0:
        values = shard_levels(own_key, extent, split, -0.22, 0.18) * values
    return jnp.clip(values, min=-most, max=most).astype(kind)


def setup_inputs(seed: int = 0) -> dict:
    splits = jax.random.split(jax.random.key(seed), 6)
    features = normal_values(splits[0], (MEMBER_COUNT, NLAT, NLON, C), 1.0, 6.0, ((0, 8), (1, 32)))
    previous = normal_values(splits[1], (MEMBER_COUNT, VARS, NLAT, NLON), 1.0, 6.0, ((0, 8), (2, 32)))
    target = normal_values(splits[2], (VARS, NLAT, NLON), 1.4, 8.0, ((1, 32),))
    weight = normal_values(splits[3], (C, VARS), C ** -0.5, 0.375)
    var_weight = jnp.clip(jnp.exp(jax.random.uniform(splits[4], (VARS,), jnp.float32, math.log(0.2), math.log(2.0))), 0.2, 2.0)
    return {"features": features, "previous": previous, "target": target, "weight": weight, "var_weight": var_weight}


smoothing = 0.1
loss_scale = 2048.0

def softened_slope(delta):
    return delta * lax.rsqrt(delta * delta + smoothing * smoothing)

def legendre_table(colatitude, orders_float, degree_count):
    cosine_col = jnp.cos(colatitude)[None, :]
    sine_col = jnp.sin(colatitude)[None, :]
    orders_col = orders_float[:, None]
    log_diag = 0.5 * (jax.scipy.special.gammaln(orders_col + 1.5) - jax.scipy.special.gammaln(orders_col + 1.0) - jax.scipy.special.gammaln(jnp.float32(1.5))) + orders_col * jnp.log(sine_col)
    diagonal_rows = jnp.exp(log_diag) * jnp.float32(math.sqrt(0.25 / math.pi))
    zero_rows = jnp.zeros_like(diagonal_rows)

    def recur_step(state_pair, degree):
        last_row, before_row = state_pair
        degree_f = degree.astype(jnp.float32)
        scale_new = jnp.sqrt(jnp.maximum(4.0 * degree_f * degree_f - 1.0, 0.0) / jnp.maximum(degree_f * degree_f - orders_col * orders_col, 1.0))
        shifted = degree_f - 1.0
        scale_old = jnp.sqrt(jnp.maximum(shifted * shifted - orders_col * orders_col, 0.0) / jnp.maximum(4.0 * shifted * shifted - 1.0, 1.0))
        recurred = scale_new * (cosine_col * last_row - scale_old * before_row)
        new_row = jnp.where(degree_f == orders_col, diagonal_rows, jnp.where(degree_f > orders_col, recurred, zero_rows))
        return ((new_row, last_row), new_row)
    final_pair, rows = lax.scan(recur_step, (zero_rows, zero_rows), jnp.arange(degree_count, dtype=jnp.int32), unroll=4)
    return rows

def reference(features, previous, target, weight, var_weight):
    colatitude = jnp.pi * (jnp.arange(NLAT, dtype=jnp.float32) + BAND_START) / (FULL_LAT - 1)
    cell_area = jnp.sin(colatitude)
    sphere_rows = jnp.sin(jnp.pi * jnp.arange(FULL_LAT, dtype=jnp.float32) / (FULL_LAT - 1))
    area_total = NLON * jnp.sum(sphere_rows)
    weight_wide = weight.astype(jnp.float32)
    projected_field = [jnp.dot(features[member_index].reshape(NLAT * NLON, C).astype(jnp.float32), weight_wide, preferred_element_type=jnp.float32).T.reshape(VARS, NLAT, NLON) for member_index in range(MEMBER_COUNT)]
    predicted_field = jnp.stack(projected_field) + previous.astype(jnp.float32)
    target_field = target.astype(jnp.float32)
    pairwise_total = jnp.zeros_like(predicted_field)
    for member_index in range(MEMBER_COUNT):
        pairwise_total = pairwise_total + softened_slope(predicted_field - predicted_field[member_index][None])
    gridpoint_scale = loss_scale * var_weight[:, None, None] * cell_area[None, :, None] / area_total
    member_gradient = (gridpoint_scale[None] * (softened_slope(predicted_field - target_field[None]) / MEMBER_COUNT - pairwise_total / (MEMBER_COUNT * (MEMBER_COUNT - 1)))).astype(jnp.bfloat16)
    weight_grad = jnp.zeros((C, VARS), jnp.float32)
    for member_index in range(MEMBER_COUNT):
        weight_grad = weight_grad + jnp.dot(member_gradient[member_index].reshape(VARS, NLAT * NLON).astype(jnp.float32), features[member_index].reshape(NLAT * NLON, C).astype(jnp.float32), preferred_element_type=jnp.float32).T
    orders_all = jnp.arange(ORDERS, dtype=jnp.int32)
    order_weight = jnp.where(orders_all == 0, 1.0, 2.0).astype(jnp.float32)
    table = legendre_table(colatitude, orders_all.astype(jnp.float32), DEGREES)

    def member_spectral(grad_rows):
        gridpoint_gradient = jnp.dot(weight_wide, grad_rows.reshape(VARS, NLAT * NLON).astype(jnp.float32), preferred_element_type=jnp.float32).T.reshape(NLAT, NLON, C)
        transformed = jnp.fft.rfft(gridpoint_gradient, axis=1)[:, :ORDERS, :]
        fourier = jnp.stack([jnp.real(transformed), jnp.imag(transformed)], axis=1) * order_weight[None, None, :, None]
        return jnp.einsum('lmi,ipmc->mlpc', table, fourier, precision=lax.Precision.HIGHEST).astype(jnp.bfloat16)
    spectral_grad = lax.map(member_spectral, member_gradient)
    return (spectral_grad, weight_grad)
```

```python
import functools
import math

import jax
import jax.numpy as jnp
import ml_dtypes
import numpy as np
from jax import lax
from jax.experimental import pallas as pl
from jax.experimental.pallas import tpu as pltpu
from jax.sharding import PartitionSpec as P

FULL_LAT = 721
DEGREES = 352
ORDERS_PER = 11
MP = 2 * ORDERS_PER
MPAD = 24
ENS = 8
ROWS = 4
NLON = 1440
LPAD = 1536
LBLK = 384
NTILE = LPAD // 128
CH = 256
NVAR = 72
VCHUNKS = ((0, 32), (32, 32), (64, 8))
WTILES = 18

smoothing = 0.1
loss_scale = 2048.0
F32 = jnp.float32
BF16 = jnp.bfloat16
MESH = pl.DeviceIdType.MESH


@functools.lru_cache(maxsize=None)
def tables(lat_count):
    rows = ROWS * lat_count
    first = (FULL_LAT - rows) // 2
    colat = np.pi * (np.arange(rows) + first) / (FULL_LAT - 1)
    total = NLON * np.sum(np.sin(np.pi * np.arange(FULL_LAT) / (FULL_LAT - 1)))
    area = np.zeros((lat_count, 8, 128), np.float32)
    area[:, :ROWS] = (loss_scale * np.sin(colat) / total).reshape(lat_count, ROWS, 1)
    order_of = (np.arange(lat_count)[None, :] * ROWS + np.arange(ROWS)[:, None]).reshape(-1)
    theta = colat[order_of]
    cosine = np.broadcast_to(np.cos(theta), (16, rows)).astype(np.float32)
    count = ORDERS_PER * lat_count
    lg = np.array([math.lgamma(m + 1.5) - math.lgamma(m + 1.0) - math.lgamma(1.5) for m in range(count)])
    diag = np.exp(0.5 * lg[:, None] + np.arange(count)[:, None] * np.log(np.sin(theta))[None, :])
    diag = diag * math.sqrt(0.25 / math.pi)
    diag_table = np.zeros((lat_count, 16, rows), np.float32)
    diag_table[:, :ORDERS_PER] = diag.reshape(lat_count, ORDERS_PER, rows)
    m = np.arange(count)
    j = np.arange(NLON)
    angle = 2.0 * np.pi / NLON * ((m[:, None] * j[None, :]) % NLON)
    ow = np.where(m == 0, 1.0, 2.0)[:, None]
    basis = np.zeros((lat_count, MPAD, LPAD))
    basis[:, 0:MP:2, :NLON] = (ow * np.cos(angle)).reshape(lat_count, ORDERS_PER, NLON)
    basis[:, 1:MP:2, :NLON] = (-ow * np.sin(angle)).reshape(lat_count, ORDERS_PER, NLON)
    basis = basis.reshape(lat_count * MPAD, LPAD).astype(ml_dtypes.bfloat16)
    return area, cosine, diag_table, basis


def softened_slope(delta):
    return delta * lax.rsqrt(delta * delta + smoothing * smoothing)


def nt_dot(a, b):
    return lax.dot_general(a, b, (((1,), (1,)), ((), ())), preferred_element_type=F32)


def first_kernel(
    nlat,
    feat, prev, tgt, wt, vw, basis, area, cosx, diag,
    r0, r1, r2, tb, wg,
    featv, prevv, tgtv, basisv, areav, diagv, prev2, tgt2, fc, fsend,
    fr0, fr1, fr2, bs0, bs1, bs2, grad, ss0, ss1, ss2, s2f, m2f,
    tgo, sco, wgp, wra, wrb, wts, wfs, wfin, tleg, t2f, t2b,
    in_sem, f_send, f_recv, b_send, b_recv, l_send, l_recv,
    wa_send, wa_recv, wb_send, wb_recv, wc_send, wc_recv, tb_sem,
):
    me_e = lax.axis_index("ens")
    me_q = lax.axis_index("lat")
    npts = ROWS * nlat
    slots = -(-WTILES // nlat)
    frecv = (fr0, fr1, fr2)
    bsend = (bs0, bs1, bs2)
    ssend = (ss0, ss1, ss2)
    rout = (r0, r1, r2)

    loads = [pltpu.make_async_copy(feat.at[0, r], featv.at[r], in_sem.at[r]) for r in range(ROWS)]
    loads.append(pltpu.make_async_copy(prev.at[0], prevv, in_sem.at[4]))
    loads.append(pltpu.make_async_copy(tgt, tgtv, in_sem.at[5]))
    loads.append(pltpu.make_async_copy(area.at[me_q], areav, in_sem.at[6]))
    loads.append(pltpu.make_async_copy(diag.at[me_q], diagv, in_sem.at[7]))
    loads.append(pltpu.make_async_copy(basis, basisv, in_sem.at[8]))
    for i in (4, 0, 1, 2, 3, 5, 6, 7, 8):
        loads[i].start()

    barrier = pltpu.get_barrier_semaphore()

    def greet_ens(s, c):
        pl.semaphore_signal(barrier, inc=1, device_id={"ens": lax.rem(me_e + s, ENS)}, device_id_type=MESH)
        return c

    def greet_lat(s, c):
        pl.semaphore_signal(barrier, inc=1, device_id={"lat": lax.rem(me_q + s, nlat)}, device_id_type=MESH)
        return c

    lax.fori_loop(1, ENS, greet_ens, 0)
    lax.fori_loop(1, nlat, greet_lat, 0)

    fc[:, LPAD - 128 : LPAD] = jnp.zeros((4 * NVAR, 128), F32)
    prev2[NTILE - 1] = jnp.zeros((4 * NVAR, 128), F32)
    loads[4].wait()

    def widen_prev(i, c):
        pair = jnp.concatenate([prevv[2 * i].astype(F32), prevv[2 * i + 1].astype(F32)], axis=0)
        for lt in range(NTILE):
            wide = min(128, NLON - 128 * lt)
            prev2[lt, pl.ds(pl.multiple_of(8 * i, 8), 8), 0:wide] = pair[:, 128 * lt : 128 * lt + wide]
        return c

    lax.fori_loop(0, NVAR // 2, widen_prev, 0)
    for r in range(ROWS):
        loads[r].wait()
        fc[NVAR * r : NVAR * (r + 1), 0:NLON] = nt_dot(wt[...], featv[r])

    pl.semaphore_wait(barrier, ENS - 1 + nlat - 1)

    my_blk = me_e // 2
    my_half = lax.rem(me_e, 2)
    for k, (v0, nv) in enumerate(VCHUNKS):
        base, nh = 4 * v0, 2 * nv
        for lt in range(NTILE):
            lanes = slice(128 * lt, 128 * lt + 128)
            parts = []
            for r in range(ROWS):
                field = fc[NVAR * r + v0 : NVAR * r + v0 + nv, lanes] + prev2[lt, pl.ds(4 * v0 + r, nv, stride=4), :]
                parts.append(field * field * field * jnp.abs(field))
            fsend[base : base + 4 * nv, lanes] = jnp.concatenate(parts, axis=0).astype(BF16)

        def block_of(dev, base=base, nh=nh):
            row = pl.multiple_of(base + lax.rem(dev, 2) * nh, 16)
            lane = pl.multiple_of((dev // 2) * LBLK, 128)
            return pl.ds(row, nh), pl.ds(lane, LBLK)

        def send_fwd(s, c, k=k, block_of=block_of):
            dev = lax.rem(me_e + s, ENS)
            rows, lanes = block_of(dev)
            pltpu.make_async_remote_copy(
                src_ref=fsend.at[rows, lanes],
                dst_ref=frecv[k].at[me_e],
                send_sem=f_send.at[k],
                recv_sem=f_recv.at[k],
                device_id={"ens": dev},
                device_id_type=MESH,
            ).start()
            return c

        lax.fori_loop(1, ENS, send_fwd, 0)
        rows, lanes = block_of(me_e)
        pltpu.make_async_copy(fsend.at[rows, lanes], frecv[k].at[me_e], f_recv.at[k]).start()

    loads[5].wait()
    tgt2[NTILE - 1] = jnp.zeros((4 * NVAR, 128), F32)

    def widen_tgt(i, c):
        pair = jnp.concatenate([tgtv[2 * i].astype(F32), tgtv[2 * i + 1].astype(F32)], axis=0)
        for lt in range(NTILE):
            wide = min(128, NLON - 128 * lt)
            tgt2[lt, pl.ds(pl.multiple_of(8 * i, 8), 8), 0:wide] = pair[:, 128 * lt : 128 * lt + wide]
        return c

    lax.fori_loop(0, NVAR // 2, widen_tgt, 0)
    loads[6].wait()
    lane_id = lax.broadcasted_iota(jnp.int32, (NVAR, NVAR), 1)
    row_id = lax.broadcasted_iota(jnp.int32, (NVAR, NVAR), 0)
    vcol = jnp.sum(jnp.where(lane_id == row_id, vw[...], 0.0), axis=1, keepdims=True)
    my_lane = pl.multiple_of(my_blk * LBLK, 128)
    for k, (v0, nv) in enumerate(VCHUNKS):
        for rr in range(2):
            r = 2 * my_half + rr
            at = 2 * v0 + rr * nv
            for i in range(3):
                tgo[at : at + nv, 128 * i : 128 * i + 128] = tgt2[3 * my_blk + i, pl.ds(4 * v0 + r, nv, stride=4), :]
            sco[at : at + nv, :] = vcol[v0 : v0 + nv] * areav[pl.ds(r, 1), :]

    loads[7].wait()
    order = (lax.broadcasted_iota(jnp.int32, (16, npts), 0) + ORDERS_PER * me_q).astype(F32)
    order_sq = order * order

    def legendre_step(l, carry):
        last, before, eps = carry
        lf = jnp.zeros((16, npts), F32) + l.astype(F32)
        lsq = lf * lf
        gap = lsq - order_sq
        ratio = jnp.maximum(gap, 1.0) / jnp.maximum(4.0 * lsq - 1.0, 1.0)
        inv = lax.rsqrt(ratio)
        new = inv * (cosx[...] * last - eps * before)
        new = jnp.where(lf == order, diagv[...], jnp.where(lf > order, new, 0.0))
        tleg[pl.ds(pl.multiple_of(16 * l, 16), 16), :] = new
        return new, last, jnp.where(gap > 0.0, ratio * inv, 0.0)

    zero = diagv[...] * 0.0
    lax.fori_loop(0, DEGREES, legendre_step, (zero, zero, zero))

    for k, (v0, nv) in enumerate(VCHUNKS):
        base, nh = 4 * v0, 2 * nv
        pltpu.make_async_copy(frecv[k], frecv[k], f_recv.at[k]).wait()

        def loss_tile(i, c, k=k, v0=v0):
            row = pl.multiple_of((i // 3) * 16, 16)
            lane = pl.multiple_of(lax.rem(i, 3) * 128, 128)
            fields = []
            for e in range(ENS):
                u = frecv[k][e, pl.ds(row, 16), pl.ds(lane, 128)].astype(F32)
                mag = lax.rsqrt(lax.rsqrt(jnp.abs(u)))
                fields.append(jnp.where(u < 0.0, -mag, mag))
            pair_sum = [None] * ENS
            for a in range(ENS):
                for b in range(a + 1, ENS):
                    s = softened_slope(fields[a] - fields[b])
                    pair_sum[a] = s if pair_sum[a] is None else pair_sum[a] + s
                    pair_sum[b] = -s if pair_sum[b] is None else pair_sum[b] - s
            at = pl.multiple_of(2 * v0 + row, 16)
            aim = tgo[pl.ds(at, 16), pl.ds(lane, 128)]
            scale = sco[pl.ds(at, 16), :]
            for e in range(ENS):
                g = softened_slope(fields[e] - aim) * (1.0 / ENS) - pair_sum[e] * (1.0 / (ENS * (ENS - 1)))
                bsend[k][e, pl.ds(row, 16), pl.ds(lane, 128)] = (scale * g).astype(BF16)
            return c

        lax.fori_loop(0, (nh // 16) * 3, loss_tile, 0)

        my_rows = pl.ds(pl.multiple_of(base + my_half * nh, 16), nh)
        my_lanes = pl.ds(my_lane, LBLK)

        def send_bwd(s, c, k=k, my_rows=my_rows, my_lanes=my_lanes):
            dev = lax.rem(me_e + s, ENS)
            pltpu.make_async_remote_copy(
                src_ref=bsend[k].at[dev],
                dst_ref=grad.at[my_rows, my_lanes],
                send_sem=b_send.at[k],
                recv_sem=b_recv.at[k],
                device_id={"ens": dev},
                device_id_type=MESH,
            ).start()
            return c

        lax.fori_loop(1, ENS, send_bwd, 0)
        pltpu.make_async_copy(bsend[k].at[me_e], grad.at[my_rows, my_lanes], b_recv.at[k]).start()

    t2f[...] = jnp.zeros((2, 2 * DEGREES, npts), F32)

    def spread(m, c):
        rows = tleg[pl.ds(m, DEGREES, stride=16), :]
        for p in range(2):
            t2f[p, pl.ds(p, DEGREES, stride=2), :] = rows
            t2b[m, :, npts * p : npts * (p + 1)] = t2f[p].astype(BF16)
        return c

    lax.fori_loop(0, ORDERS_PER, spread, 0)
    pltpu.make_async_copy(t2b, tb, tb_sem).start()

    loads[8].wait()
    m2f[...] = jnp.zeros(m2f.shape, F32)
    for k, (v0, nv) in enumerate(VCHUNKS):
        base = 4 * v0
        rows = pl.ds(base, 4 * nv)
        pltpu.make_async_copy(grad.at[rows, :], grad.at[rows, :], b_recv.at[k]).wait()

        wsum = None
        for r in range(ROWS):
            if nv % 16 == 0:
                g = grad[base + r * nv : base + (r + 1) * nv, 0:NLON]
            else:
                pair = grad[base + (r // 2) * 2 * nv : base + (r // 2 + 1) * 2 * nv, 0:NLON]
                g = pair.astype(F32)[(r % 2) * nv : (r % 2 + 1) * nv].astype(BF16)
            term = jnp.dot(g, featv[r], preferred_element_type=F32)
            wsum = term if wsum is None else wsum + term
        wgp[v0 : v0 + nv, :] = wsum
        for t in range(2 * (v0 // 8), 2 * ((v0 + nv) // 8)):
            tile = wgp.at[pl.ds(8 * (t // 2), 8), pl.ds(128 * (t % 2), 128)]
            slot, owner = t // nlat, t % nlat

            @pl.when(me_q == owner)
            def _(tile=tile, slot=slot):
                pltpu.make_async_copy(tile, wra.at[slot, me_q], wa_recv.at[slot]).start()

            @pl.when(me_q != owner)
            def _(tile=tile, slot=slot, owner=owner, t=t):
                pltpu.make_async_remote_copy(
                    src_ref=tile,
                    dst_ref=wra.at[slot, me_q],
                    send_sem=wa_send.at[t],
                    recv_sem=wa_recv.at[slot],
                    device_id={"lat": jnp.int32(owner)},
                    device_id_type=MESH,
                ).start()

        waves = nt_dot(basisv[...], grad[rows, :])
        if k < 2:
            ssend[k][...] = waves.reshape(nlat, MPAD, 128).astype(BF16)
        else:
            s2f[:, 0:32] = waves
            for j in range(6):
                cols = [s2f[pl.ds(6 * g + j, nlat, stride=MPAD), :][:, 0:32] for g in range(4)]
                m2f[pl.ds(j, nlat, stride=8), :] = jnp.concatenate(cols, axis=1)
            ssend[k][...] = m2f[...].reshape(nlat, 8, 128).astype(BF16)

        def send_lat(s, c, k=k):
            dev = lax.rem(me_q + s, nlat)
            pltpu.make_async_remote_copy(
                src_ref=ssend[k].at[dev],
                dst_ref=rout[k].at[me_q],
                send_sem=l_send.at[k],
                recv_sem=l_recv.at[k],
                device_id={"lat": dev},
                device_id_type=MESH,
            ).start()
            return c

        lax.fori_loop(1, nlat, send_lat, 0)
        pltpu.make_async_copy(ssend[k].at[me_q], rout[k].at[me_q], l_recv.at[k]).start()

    for slot in range(slots):
        t = slot * nlat + me_q

        @pl.when(t < WTILES)
        def _(slot=slot):
            pltpu.make_async_copy(wra.at[slot], wra.at[slot], wa_recv.at[slot]).wait()
            wts[slot] = jnp.sum(wra[slot], axis=0)

            def send_ens(s, c):
                pltpu.make_async_remote_copy(
                    src_ref=wts.at[slot],
                    dst_ref=wrb.at[slot, me_e],
                    send_sem=wb_send.at[slot],
                    recv_sem=wb_recv.at[slot],
                    device_id={"ens": lax.rem(me_e + s, ENS)},
                    device_id_type=MESH,
                ).start()
                return c

            lax.fori_loop(1, ENS, send_ens, 0)
            pltpu.make_async_copy(wts.at[slot], wrb.at[slot, me_e], wb_recv.at[slot]).start()

    for slot in range(slots):
        t = slot * nlat + me_q

        @pl.when(t < WTILES)
        def _(slot=slot, t=t):
            pltpu.make_async_copy(wrb.at[slot], wrb.at[slot], wb_recv.at[slot]).wait()
            wfs[slot] = jnp.sum(wrb[slot], axis=0)

            def send_back(s, c):
                pltpu.make_async_remote_copy(
                    src_ref=wfs.at[slot],
                    dst_ref=wfin.at[t],
                    send_sem=wc_send.at[slot],
                    recv_sem=wc_recv,
                    device_id={"lat": lax.rem(me_q + s, nlat)},
                    device_id_type=MESH,
                ).start()
                return c

            lax.fori_loop(1, nlat, send_back, 0)
            pltpu.make_async_copy(wfs.at[slot], wfin.at[t], wc_recv).start()

    pltpu.make_async_copy(wfin, wfin, wc_recv).wait()
    for t in range(WTILES):
        wg[8 * (t // 2) : 8 * (t // 2) + 8, 128 * (t % 2) : 128 * (t % 2) + 128] = wfin[t]

    for k in range(3):
        pltpu.make_async_copy(rout[k], rout[k], l_recv.at[k]).wait()
    for k in range(3):
        part = frecv[k].at[pl.ds(0, ENS - 1)]
        pltpu.make_async_copy(part, part, f_send.at[k]).wait()
        part = bsend[k].at[pl.ds(0, ENS - 1)]
        pltpu.make_async_copy(part, part, b_send.at[k]).wait()
        part = ssend[k].at[pl.ds(0, nlat - 1)]
        pltpu.make_async_copy(part, part, l_send.at[k]).wait()
    for t in range(WTILES):
        slot, owner = t // nlat, t % nlat

        @pl.when(me_q != owner)
        def _(t=t):
            tile = wgp.at[pl.ds(8 * (t // 2), 8), pl.ds(128 * (t % 2), 128)]
            pltpu.make_async_copy(tile, tile, wa_send.at[t]).wait()

    for slot in range(slots):

        @pl.when(slot * nlat + me_q < WTILES)
        def _(slot=slot):
            part = wrb.at[slot, pl.ds(0, ENS - 1)]
            pltpu.make_async_copy(part, part, wb_send.at[slot]).wait()
            part = wra.at[slot, pl.ds(0, nlat - 1)]
            pltpu.make_async_copy(part, part, wc_send.at[slot]).wait()

    pltpu.make_async_copy(t2b, tb, tb_sem).wait()


def second_kernel(nlat, r0, r1, r2, wt, tb, out, x01, x2f, bd01, bd2f, bd2, lhs01, lhs2, ybuf):
    @pl.when(pl.program_id(0) == 0)
    def _():
        x01[0] = r0[...].astype(F32).reshape(nlat * MPAD, 128)
        x01[1] = r1[...].astype(F32).reshape(nlat * MPAD, 128)
        x2f[...] = r2[...].astype(F32).reshape(nlat * 8, 128)
        bd01[...] = jnp.zeros(bd01.shape, BF16)
        bd2f[...] = jnp.zeros(bd2f.shape, F32)
        tail = wt[64:72, :].astype(F32)
        for r in range(ROWS):
            for k in range(2):
                bd01[128 * k + 32 * r : 128 * k + 32 * r + 32, CH * r : CH * r + CH] = wt[32 * k : 32 * k + 32, :]
            for g in range(4):
                bd2f[32 * g + 8 * r : 32 * g + 8 * r + 8, CH * r : CH * r + CH] = tail
        bd2[...] = bd2f[...].astype(BF16)
        for i in range(MP):
            for k in range(2):
                lhs01[nlat * i : nlat * (i + 1), 128 * k : 128 * k + 128] = x01[k, pl.ds(i, nlat, stride=MPAD), :].astype(BF16)
        for j in range(6):
            lhs2[nlat * j : nlat * (j + 1), :] = x2f[pl.ds(j, nlat, stride=8), :]
        for g in range(4):
            nj = min(6, MP - 6 * g)
            n = nj * nlat
            group = lax.broadcasted_iota(jnp.int32, (n, 128), 1) // 32
            last = jnp.where(group == g, lhs2[0:n, :], 0.0).astype(BF16)
            y = jnp.dot(lhs01[6 * g * nlat : 6 * g * nlat + n, :], bd01[...], preferred_element_type=F32)
            y = y + jnp.dot(last, bd2[...], preferred_element_type=F32)
            for j in range(nj):
                m, p = (6 * g + j) // 2, (6 * g + j) % 2
                for r in range(ROWS):
                    at = (p * ROWS + r) * nlat
                    ybuf[m, at : at + nlat, :] = y[j * nlat : (j + 1) * nlat, CH * r : CH * r + CH].astype(BF16)

    res = jnp.dot(tb[0], ybuf[pl.program_id(0)], preferred_element_type=F32).astype(BF16)
    out[0, 0] = res.reshape(DEGREES, 2, CH)


def local(nlat, features, previous, target, weight, var_weight):
    area, cosine, diag, basis = tables(nlat)
    npts = ROWS * nlat
    slots = -(-WTILES // nlat)
    any_spec = pl.BlockSpec(memory_space=pl.ANY)
    vmem = pl.BlockSpec(memory_space=pltpu.VMEM)
    wt = weight.T
    dma = pltpu.SemaphoreType.DMA
    chunk_rows = [2 * nv for _, nv in VCHUNKS]
    r0, r1, r2, tb, wg = pl.pallas_call(
        functools.partial(first_kernel, nlat),
        out_shape=[
            jax.ShapeDtypeStruct((nlat, MPAD, 128), BF16),
            jax.ShapeDtypeStruct((nlat, MPAD, 128), BF16),
            jax.ShapeDtypeStruct((nlat, 8, 128), BF16),
            jax.ShapeDtypeStruct((ORDERS_PER, 2 * DEGREES, 2 * npts), BF16),
            jax.ShapeDtypeStruct((NVAR, CH), F32),
        ],
        in_specs=[any_spec] * 3 + [vmem] * 2 + [any_spec] * 2 + [vmem] + [any_spec],
        out_specs=[any_spec] * 4 + [vmem],
        scratch_shapes=[
            pltpu.VMEM((ROWS, NLON, CH), BF16),
            pltpu.VMEM((NVAR, ROWS, NLON), BF16),
            pltpu.VMEM((NVAR, ROWS, NLON), BF16),
            pltpu.VMEM((nlat * MPAD, LPAD), BF16),
            pltpu.VMEM((8, 128), F32),
            pltpu.VMEM((16, npts), F32),
            pltpu.VMEM((NTILE, 4 * NVAR, 128), F32),
            pltpu.VMEM((NTILE, 4 * NVAR, 128), F32),
            pltpu.VMEM((4 * NVAR, LPAD), F32),
            pltpu.VMEM((4 * NVAR, LPAD), BF16),
        ]
        + [pltpu.VMEM((ENS, n, LBLK), BF16) for n in chunk_rows] * 2
        + [
            pltpu.VMEM((4 * NVAR, LPAD), BF16),
            pltpu.VMEM((nlat, MPAD, 128), BF16),
            pltpu.VMEM((nlat, MPAD, 128), BF16),
            pltpu.VMEM((nlat, 8, 128), BF16),
            pltpu.VMEM((nlat * MPAD, 128), F32),
            pltpu.VMEM((nlat * 8, 128), F32),
            pltpu.VMEM((2 * NVAR, LBLK), F32),
            pltpu.VMEM((2 * NVAR, 128), F32),
            pltpu.VMEM((NVAR, CH), F32),
            pltpu.VMEM((slots, nlat, 8, 128), F32),
            pltpu.VMEM((slots, ENS, 8, 128), F32),
            pltpu.VMEM((slots, 8, 128), F32),
            pltpu.VMEM((slots, 8, 128), F32),
            pltpu.VMEM((WTILES, 8, 128), F32),
            pltpu.VMEM((DEGREES * 16, npts), F32),
            pltpu.VMEM((2, 2 * DEGREES, npts), F32),
            pltpu.VMEM((ORDERS_PER, 2 * DEGREES, 2 * npts), BF16),
            dma((9,)), dma((3,)), dma((3,)), dma((3,)), dma((3,)), dma((3,)), dma((3,)),
            dma((WTILES,)), dma((slots,)), dma((slots,)), dma((slots,)), dma((slots,)), dma, dma,
        ],
        compiler_params=pltpu.CompilerParams(
            collective_id=0, has_side_effects=True, vmem_limit_bytes=48 * 1024 * 1024
        ),
        name="loss_and_transform",
    )(features, previous, target, wt, var_weight.reshape(1, NVAR),
      jnp.asarray(basis), jnp.asarray(area), jnp.asarray(cosine), jnp.asarray(diag))

    full = lambda shape: pl.BlockSpec(shape, lambda i: (0,) * len(shape))
    spectral = pl.pallas_call(
        functools.partial(second_kernel, nlat),
        grid=(ORDERS_PER,),
        out_shape=jax.ShapeDtypeStruct((1, ORDERS_PER, DEGREES, 2, CH), BF16),
        in_specs=[
            full((nlat, MPAD, 128)),
            full((nlat, MPAD, 128)),
            full((nlat, 8, 128)),
            full((NVAR, CH)),
            pl.BlockSpec((1, 2 * DEGREES, 2 * npts), lambda i: (i, 0, 0)),
        ],
        out_specs=pl.BlockSpec((1, 1, DEGREES, 2, CH), lambda i: (0, i, 0, 0, 0)),
        scratch_shapes=[
            pltpu.VMEM((2, nlat * MPAD, 128), F32),
            pltpu.VMEM((nlat * 8, 128), F32),
            pltpu.VMEM((256, ROWS * CH), BF16),
            pltpu.VMEM((128, ROWS * CH), F32),
            pltpu.VMEM((128, ROWS * CH), BF16),
            pltpu.VMEM((nlat * MP, 256), BF16),
            pltpu.VMEM((nlat * 6, 128), F32),
            pltpu.VMEM((ORDERS_PER, 2 * npts, CH), BF16),
        ],
        compiler_params=pltpu.CompilerParams(vmem_limit_bytes=32 * 1024 * 1024),
        name="latitude_transform",
    )(r0, r1, r2, wt, tb)
    return spectral, wg.T


def solution(mesh):
    placed = (
        P("ens", "lat", None, None),
        P("ens", None, "lat", None),
        P(None, "lat", None),
        P(),
        P(),
    )
    return jax.shard_map(
        functools.partial(local, mesh.shape["lat"]),
        mesh=mesh,
        in_specs=placed,
        out_specs=(P("ens", "lat", None, None, None), P()),
        check_vma=False,
    )
```

```python
import functools
import math

import jax
import jax.numpy as jnp
import ml_dtypes
import numpy as np
from jax import lax
from jax.experimental import pallas as pl
from jax.experimental.pallas import tpu as pltpu
from jax.sharding import PartitionSpec as P

FULL_LAT = 721
DEGREES = 352
ORDERS_PER = 11
MP = 2 * ORDERS_PER
MPAD = 24
ENS = 8
ROWS = 4
NLON = 1440
LPAD = 1536
LBLK = 384
NTILE = LPAD // 128
CH = 256
NVAR = 72
VCHUNKS = ((0, 32), (32, 32), (64, 8))

smoothing = 0.1
loss_scale = 2048.0
F32 = jnp.float32
BF16 = jnp.bfloat16
MESH = pl.DeviceIdType.MESH


@functools.lru_cache(maxsize=None)
def tables(lat_count):
    rows = ROWS * lat_count
    first = (FULL_LAT - rows) // 2
    colat = np.pi * (np.arange(rows) + first) / (FULL_LAT - 1)
    total = NLON * np.sum(np.sin(np.pi * np.arange(FULL_LAT) / (FULL_LAT - 1)))
    area = np.zeros((lat_count, 8, 128), np.float32)
    area[:, :ROWS] = (loss_scale * np.sin(colat) / total).reshape(lat_count, ROWS, 1)
    order_of = (np.arange(lat_count)[None, :] * ROWS + np.arange(ROWS)[:, None]).reshape(-1)
    theta = colat[order_of]
    cosine = np.broadcast_to(np.cos(theta), (16, rows)).astype(np.float32)
    count = ORDERS_PER * lat_count
    lg = np.array([math.lgamma(m + 1.5) - math.lgamma(m + 1.0) - math.lgamma(1.5) for m in range(count)])
    diag = np.exp(0.5 * lg[:, None] + np.arange(count)[:, None] * np.log(np.sin(theta))[None, :])
    diag = diag * math.sqrt(0.25 / math.pi)
    diag_table = np.zeros((lat_count, 16, rows), np.float32)
    diag_table[:, :ORDERS_PER] = diag.reshape(lat_count, ORDERS_PER, rows)
    m = np.arange(count)
    j = np.arange(NLON)
    angle = 2.0 * np.pi / NLON * ((m[:, None] * j[None, :]) % NLON)
    ow = np.where(m == 0, 1.0, 2.0)[:, None]
    basis = np.zeros((lat_count, MPAD, LPAD))
    basis[:, 0:MP:2, :NLON] = (ow * np.cos(angle)).reshape(lat_count, ORDERS_PER, NLON)
    basis[:, 1:MP:2, :NLON] = (-ow * np.sin(angle)).reshape(lat_count, ORDERS_PER, NLON)
    basis = basis.reshape(lat_count * MPAD, LPAD).astype(ml_dtypes.bfloat16)
    return area, cosine, diag_table, basis


def softened_slope(delta):
    return delta * lax.rsqrt(delta * delta + smoothing * smoothing)


def nt_dot(a, b):
    return lax.dot_general(a, b, (((1,), (1,)), ((), ())), preferred_element_type=F32)


def first_kernel(
    nlat,
    feat, prev, tgt, wt, vw, basis, area, cosx, diag,
    yb, tb, wg,
    featv, prevv, tgtv, basisv, areav, diagv, prev2, tgt2, fc, fsend,
    fr0, fr1, fr2, bs0, bs1, bs2, grad, ss0, ss1, ss2, rv0, rv1, rv2, s2f, m2f,
    tgo, sco, wgp, wsum, wa, wb, wc, wd, wx, wy, wz, tleg, tbv,
    x01, x2f, bd01, bd2f, bd2, lhs01, lhs2, ybuf,
    in_sem, f_send, f_recv, b_send, b_recv, l_send, l_recv, w_send, w_recv, out_sem,
):
    me_e = lax.axis_index("ens")
    me_q = lax.axis_index("lat")
    npts = ROWS * nlat
    n4 = min(4, nlat)
    nz = nlat // n4
    me_z, me_4 = me_q // n4, lax.rem(me_q, n4)
    frecv = (fr0, fr1, fr2)
    bsend = (bs0, bs1, bs2)
    ssend = (ss0, ss1, ss2)
    rout = (rv0, rv1, rv2)

    loads = [pltpu.make_async_copy(feat.at[0, r], featv.at[r], in_sem.at[r]) for r in range(ROWS)]
    loads.append(pltpu.make_async_copy(prev.at[0], prevv, in_sem.at[4]))
    loads.append(pltpu.make_async_copy(tgt, tgtv, in_sem.at[5]))
    loads.append(pltpu.make_async_copy(area.at[me_q], areav, in_sem.at[6]))
    loads.append(pltpu.make_async_copy(diag.at[me_q], diagv, in_sem.at[7]))
    loads.append(pltpu.make_async_copy(basis, basisv, in_sem.at[8]))
    for i in (4, 0, 1, 2, 3, 5, 6, 7, 8):
        loads[i].start()

    barrier = pltpu.get_barrier_semaphore()

    def greet_ens(s, c):
        pl.semaphore_signal(barrier, inc=1, device_id={"ens": lax.rem(me_e + s, ENS)}, device_id_type=MESH)
        return c

    def greet_lat(s, c):
        pl.semaphore_signal(barrier, inc=1, device_id={"lat": lax.rem(me_q + s, nlat)}, device_id_type=MESH)
        return c

    lax.fori_loop(1, ENS, greet_ens, 0)
    lax.fori_loop(1, nlat, greet_lat, 0)

    fc[:, LPAD - 128 : LPAD] = jnp.zeros((4 * NVAR, 128), F32)
    prev2[NTILE - 1] = jnp.zeros((4 * NVAR, 128), F32)
    loads[4].wait()

    def widen_prev(i, c):
        pair = jnp.concatenate([prevv[2 * i].astype(F32), prevv[2 * i + 1].astype(F32)], axis=0)
        for lt in range(NTILE):
            wide = min(128, NLON - 128 * lt)
            prev2[lt, pl.ds(pl.multiple_of(8 * i, 8), 8), 0:wide] = pair[:, 128 * lt : 128 * lt + wide]
        return c

    lax.fori_loop(0, NVAR // 2, widen_prev, 0)
    for r in range(ROWS):
        loads[r].wait()
        fc[NVAR * r : NVAR * (r + 1), 0:NLON] = nt_dot(wt[...], featv[r])

    pl.semaphore_wait(barrier, ENS - 1 + nlat - 1)

    my_blk = me_e // 2
    my_half = lax.rem(me_e, 2)
    for k, (v0, nv) in enumerate(VCHUNKS):
        base, nh = 4 * v0, 2 * nv
        for lt in range(NTILE):
            lanes = slice(128 * lt, 128 * lt + 128)
            parts = []
            for r in range(ROWS):
                field = fc[NVAR * r + v0 : NVAR * r + v0 + nv, lanes] + prev2[lt, pl.ds(4 * v0 + r, nv, stride=4), :]
                parts.append(field * field * field * jnp.abs(field))
            fsend[base : base + 4 * nv, lanes] = jnp.concatenate(parts, axis=0).astype(BF16)

        def block_of(dev, base=base, nh=nh):
            row = pl.multiple_of(base + lax.rem(dev, 2) * nh, 16)
            lane = pl.multiple_of((dev // 2) * LBLK, 128)
            return pl.ds(row, nh), pl.ds(lane, LBLK)

        def send_fwd(s, c, k=k, block_of=block_of):
            dev = lax.rem(me_e + s, ENS)
            rows, lanes = block_of(dev)
            pltpu.make_async_remote_copy(
                src_ref=fsend.at[rows, lanes],
                dst_ref=frecv[k].at[me_e],
                send_sem=f_send.at[k],
                recv_sem=f_recv.at[k],
                device_id={"ens": dev},
                device_id_type=MESH,
            ).start()
            return c

        lax.fori_loop(1, ENS, send_fwd, 0)
        rows, lanes = block_of(me_e)
        pltpu.make_async_copy(fsend.at[rows, lanes], frecv[k].at[me_e], f_recv.at[k]).start()

    loads[5].wait()
    tgt2[NTILE - 1] = jnp.zeros((4 * NVAR, 128), F32)

    def widen_tgt(i, c):
        pair = jnp.concatenate([tgtv[2 * i].astype(F32), tgtv[2 * i + 1].astype(F32)], axis=0)
        for lt in range(NTILE):
            wide = min(128, NLON - 128 * lt)
            tgt2[lt, pl.ds(pl.multiple_of(8 * i, 8), 8), 0:wide] = pair[:, 128 * lt : 128 * lt + wide]
        return c

    lax.fori_loop(0, NVAR // 2, widen_tgt, 0)
    loads[6].wait()
    lane_id = lax.broadcasted_iota(jnp.int32, (NVAR, NVAR), 1)
    row_id = lax.broadcasted_iota(jnp.int32, (NVAR, NVAR), 0)
    vcol = jnp.sum(jnp.where(lane_id == row_id, vw[...], 0.0), axis=1, keepdims=True)
    my_lane = pl.multiple_of(my_blk * LBLK, 128)
    for k, (v0, nv) in enumerate(VCHUNKS):
        for rr in range(2):
            r = 2 * my_half + rr
            at = 2 * v0 + rr * nv
            for i in range(3):
                tgo[at : at + nv, 128 * i : 128 * i + 128] = tgt2[3 * my_blk + i, pl.ds(4 * v0 + r, nv, stride=4), :]
            sco[at : at + nv, :] = vcol[v0 : v0 + nv] * areav[pl.ds(r, 1), :]

    loads[7].wait()
    order = (lax.broadcasted_iota(jnp.int32, (16, npts), 0) + ORDERS_PER * me_q).astype(F32)
    order_sq = order * order

    def legendre_step(l, carry):
        last, before, eps = carry
        lf = jnp.zeros((16, npts), F32) + l.astype(F32)
        lsq = lf * lf
        gap = lsq - order_sq
        ratio = jnp.maximum(gap, 1.0) / jnp.maximum(4.0 * lsq - 1.0, 1.0)
        inv = lax.rsqrt(ratio)
        new = inv * (cosx[...] * last - eps * before)
        new = jnp.where(lf == order, diagv[...], jnp.where(lf > order, new, 0.0))
        tleg[pl.ds(pl.multiple_of(16 * l, 16), 16), :] = new
        return new, last, jnp.where(gap > 0.0, ratio * inv, 0.0)

    zero = diagv[...] * 0.0
    lax.fori_loop(0, DEGREES, legendre_step, (zero, zero, zero))

    for k, (v0, nv) in enumerate(VCHUNKS):
        base, nh = 4 * v0, 2 * nv
        pltpu.make_async_copy(frecv[k], frecv[k], f_recv.at[k]).wait()

        def loss_tile(i, c, k=k, v0=v0):
            row = pl.multiple_of((i // 3) * 16, 16)
            lane = pl.multiple_of(lax.rem(i, 3) * 128, 128)
            fields = []
            for e in range(ENS):
                u = frecv[k][e, pl.ds(row, 16), pl.ds(lane, 128)].astype(F32)
                mag = lax.rsqrt(lax.rsqrt(jnp.abs(u)))
                fields.append(jnp.where(u < 0.0, -mag, mag))
            pair_sum = [None] * ENS
            for a in range(ENS):
                for b in range(a + 1, ENS):
                    s = softened_slope(fields[a] - fields[b])
                    pair_sum[a] = s if pair_sum[a] is None else pair_sum[a] + s
                    pair_sum[b] = -s if pair_sum[b] is None else pair_sum[b] - s
            at = pl.multiple_of(2 * v0 + row, 16)
            aim = tgo[pl.ds(at, 16), pl.ds(lane, 128)]
            scale = sco[pl.ds(at, 16), :]
            for e in range(ENS):
                g = softened_slope(fields[e] - aim) * (1.0 / ENS) - pair_sum[e] * (1.0 / (ENS * (ENS - 1)))
                bsend[k][e, pl.ds(row, 16), pl.ds(lane, 128)] = (scale * g).astype(BF16)
            return c

        lax.fori_loop(0, (nh // 16) * 3, loss_tile, 0)

        my_rows = pl.ds(pl.multiple_of(base + my_half * nh, 16), nh)
        my_lanes = pl.ds(my_lane, LBLK)

        def send_bwd(s, c, k=k, my_rows=my_rows, my_lanes=my_lanes):
            dev = lax.rem(me_e + s, ENS)
            pltpu.make_async_remote_copy(
                src_ref=bsend[k].at[dev],
                dst_ref=grad.at[my_rows, my_lanes],
                send_sem=b_send.at[k],
                recv_sem=b_recv.at[k],
                device_id={"ens": dev},
                device_id_type=MESH,
            ).start()
            return c

        lax.fori_loop(1, ENS, send_bwd, 0)
        pltpu.make_async_copy(bsend[k].at[me_e], grad.at[my_rows, my_lanes], b_recv.at[k]).start()

    def regroup(m, c):
        tbv[m] = tleg[pl.ds(m, DEGREES, stride=16), :].astype(BF16)
        return c

    lax.fori_loop(0, ORDERS_PER, regroup, 0)
    pltpu.make_async_copy(tbv, tb, out_sem.at[0]).start()

    bd01[...] = jnp.zeros(bd01.shape, BF16)
    bd2f[...] = jnp.zeros(bd2f.shape, F32)
    tail = wt[64:72, :].astype(F32)
    for r in range(ROWS):
        for k in range(2):
            bd01[128 * k + 32 * r : 128 * k + 32 * r + 32, CH * r : CH * r + CH] = wt[32 * k : 32 * k + 32, :]
        for g in range(4):
            bd2f[32 * g + 8 * r : 32 * g + 8 * r + 8, CH * r : CH * r + CH] = tail
    bd2[...] = bd2f[...].astype(BF16)

    def over_z(src, dst, i):
        def send(s, c):
            z = lax.rem(me_z + s, nz)
            pltpu.make_async_remote_copy(
                src_ref=src(z),
                dst_ref=dst.at[me_z],
                send_sem=w_send.at[i],
                recv_sem=w_recv.at[i],
                device_id={"lat": z * n4 + me_4},
                device_id_type=MESH,
            ).start()
            return c

        lax.fori_loop(1, nz, send, 0)
        pltpu.make_async_copy(src(me_z), dst.at[me_z], w_recv.at[i]).start()

    def over_4(src, dst, i):
        def send(s, c):
            pltpu.make_async_remote_copy(
                src_ref=src,
                dst_ref=dst.at[me_4],
                send_sem=w_send.at[i],
                recv_sem=w_recv.at[i],
                device_id={"lat": me_z * n4 + lax.rem(me_4 + s, n4)},
                device_id_type=MESH,
            ).start()
            return c

        lax.fori_loop(1, n4, send, 0)
        pltpu.make_async_copy(src, dst.at[me_4], w_recv.at[i]).start()

    def over_ens(src, dst, i):
        def send(s, c):
            pltpu.make_async_remote_copy(
                src_ref=src,
                dst_ref=dst.at[me_e],
                send_sem=w_send.at[i],
                recv_sem=w_recv.at[i],
                device_id={"ens": lax.rem(me_e + s, ENS)},
                device_id_type=MESH,
            ).start()
            return c

        lax.fori_loop(1, ENS, send, 0)
        pltpu.make_async_copy(src, dst.at[me_e], w_recv.at[i]).start()

    def arrived(ref, i):
        pltpu.make_async_copy(ref, ref, w_recv.at[i]).wait()
        return jnp.sum(ref[...], axis=0)

    piece = 64 // nz

    loads[8].wait()
    m2f[...] = jnp.zeros(m2f.shape, F32)
    for k, (v0, nv) in enumerate(VCHUNKS):
        base = 4 * v0
        rows = pl.ds(base, 4 * nv)
        pltpu.make_async_copy(grad.at[rows, :], grad.at[rows, :], b_recv.at[k]).wait()

        total = None
        for r in range(ROWS):
            if nv % 16 == 0:
                g = grad[base + r * nv : base + (r + 1) * nv, 0:NLON]
            else:
                pair = grad[base + (r // 2) * 2 * nv : base + (r // 2 + 1) * 2 * nv, 0:NLON]
                g = pair.astype(F32)[(r % 2) * nv : (r % 2 + 1) * nv].astype(BF16)
            term = jnp.dot(g, featv[r], preferred_element_type=F32)
            total = term if total is None else total + term
        wgp[v0 : v0 + nv, :] = total
        if k == 1:
            over_z(lambda z: wgp.at[pl.ds(pl.multiple_of(z * piece, 8), piece)], wa, 0)
        if k == 2:
            over_z(lambda z: wgp.at[pl.ds(64, 8)], wx, 4)

        waves = nt_dot(basisv[...], grad[rows, :])
        if k < 2:
            ssend[k][...] = waves.reshape(nlat, MPAD, 128).astype(BF16)
        else:
            s2f[:, 0:32] = waves
            for j in range(6):
                cols = [s2f[pl.ds(6 * g + j, nlat, stride=MPAD), :][:, 0:32] for g in range(4)]
                m2f[pl.ds(j, nlat, stride=8), :] = jnp.concatenate(cols, axis=1)
            ssend[k][...] = m2f[...].reshape(nlat, 8, 128).astype(BF16)

        def send_lat(s, c, k=k):
            dev = lax.rem(me_q + s, nlat)
            pltpu.make_async_remote_copy(
                src_ref=ssend[k].at[dev],
                dst_ref=rout[k].at[me_q],
                send_sem=l_send.at[k],
                recv_sem=l_recv.at[k],
                device_id={"lat": dev},
                device_id_type=MESH,
            ).start()
            return c

        lax.fori_loop(1, nlat, send_lat, 0)
        pltpu.make_async_copy(ssend[k].at[me_q], rout[k].at[me_q], l_recv.at[k]).start()

        if k == 1:
            wsum[0, 0:piece] = arrived(wa, 0)
            over_4(wsum.at[0, pl.ds(0, piece)], wb, 1)

    wsum[1, 0:piece] = arrived(wb, 1)
    over_ens(wsum.at[1, pl.ds(0, piece)], wc, 2)
    wsum[3, 0:8] = arrived(wx, 4)
    over_4(wsum.at[3, pl.ds(0, 8)], wy, 5)

    def gather(k):
        pltpu.make_async_copy(rout[k], rout[k], l_recv.at[k]).wait()
        if k == 2:
            x2f[...] = rout[k][...].astype(F32).reshape(nlat * 8, 128)
            for j in range(6):
                lhs2[nlat * j : nlat * (j + 1), :] = x2f[pl.ds(j, nlat, stride=8), :]
        else:
            x01[k] = rout[k][...].astype(F32).reshape(nlat * MPAD, 128)
            for i in range(MP):
                lhs01[nlat * i : nlat * (i + 1), 128 * k : 128 * k + 128] = x01[k, pl.ds(i, nlat, stride=MPAD), :].astype(BF16)

    gather(0)
    wsum[2, 0:piece] = arrived(wc, 2)
    over_z(lambda z: wsum.at[2, pl.ds(0, piece)], wd, 3)
    wsum[4, 0:8] = arrived(wy, 5)
    over_ens(wsum.at[4, pl.ds(0, 8)], wz, 6)
    gather(1)
    gather(2)
    for g in range(4):
        nj = min(6, MP - 6 * g)
        n = nj * nlat
        group = lax.broadcasted_iota(jnp.int32, (n, 128), 1) // 32
        last = jnp.where(group == g, lhs2[0:n, :], 0.0).astype(BF16)
        y = jnp.dot(lhs01[6 * g * nlat : 6 * g * nlat + n, :], bd01[...], preferred_element_type=F32)
        y = y + jnp.dot(last, bd2[...], preferred_element_type=F32)
        for j in range(nj):
            m, p = (6 * g + j) // 2, (6 * g + j) % 2
            for r in range(ROWS):
                block = y[j * nlat : (j + 1) * nlat, CH * r : CH * r + CH]
                ybuf[m, r * nlat : (r + 1) * nlat, CH * p : CH * p + CH] = block.astype(BF16)
    pltpu.make_async_copy(ybuf, yb, out_sem.at[1]).start()

    pltpu.make_async_copy(wd, wd, w_recv.at[3]).wait()
    wg[0:64, :] = wd[...].reshape(64, CH)
    wg[64:72, :] = arrived(wz, 6)

    for k in range(3):
        part = frecv[k].at[pl.ds(0, ENS - 1)]
        pltpu.make_async_copy(part, part, f_send.at[k]).wait()
        part = bsend[k].at[pl.ds(0, ENS - 1)]
        pltpu.make_async_copy(part, part, b_send.at[k]).wait()
        part = ssend[k].at[pl.ds(0, nlat - 1)]
        pltpu.make_async_copy(part, part, l_send.at[k]).wait()
    for i, (ref, n) in enumerate(((wa, nz), (wb, n4), (wc, ENS), (wd, nz), (wx, nz), (wy, n4), (wz, ENS))):
        if n > 1:
            part = ref.at[pl.ds(0, n - 1)]
            pltpu.make_async_copy(part, part, w_send.at[i]).wait()
    pltpu.make_async_copy(tbv, tb, out_sem.at[0]).wait()
    pltpu.make_async_copy(ybuf, yb, out_sem.at[1]).wait()


def second_kernel(tb, yb, wg, out, wg_out, tv, yv, ov, flat, t_sem, y_sem, o_sem, w_sem):
    for m in range(ORDERS_PER):
        pltpu.make_async_copy(yb.at[m], yv.at[m], y_sem.at[m]).start()
        pltpu.make_async_copy(tb.at[m], tv.at[m], t_sem.at[m]).start()
    passed = pltpu.make_async_copy(wg, wg_out, w_sem)
    passed.start()
    for m in range(ORDERS_PER):
        pltpu.make_async_copy(yb.at[m], yv.at[m], y_sem.at[m]).wait()
        pltpu.make_async_copy(tb.at[m], tv.at[m], t_sem.at[m]).wait()
        res = jnp.dot(tv[m], yv[m], preferred_element_type=F32)
        for p in range(2):
            for h in range(2):
                at = CH * p + 128 * h
                flat[m % 2, h, pl.ds(p, DEGREES, stride=2), :] = res[:, at : at + 128]
        rows = ov.at[m].reshape(2 * DEGREES, CH)
        for h in range(2):
            rows[:, 128 * h : 128 * h + 128] = flat[m % 2, h].astype(BF16)
        pltpu.make_async_copy(ov.at[m], out.at[0, m], o_sem.at[m]).start()
    for m in range(ORDERS_PER):
        pltpu.make_async_copy(ov.at[m], out.at[0, m], o_sem.at[m]).wait()
    passed.wait()


def local(nlat, features, previous, target, weight, var_weight):
    area, cosine, diag, basis = tables(nlat)
    npts = ROWS * nlat
    n4 = min(4, nlat)
    nz = nlat // n4
    piece = 64 // nz
    any_spec = pl.BlockSpec(memory_space=pl.ANY)
    vmem = pl.BlockSpec(memory_space=pltpu.VMEM)
    wt = weight.T
    dma = pltpu.SemaphoreType.DMA
    chunk_rows = [2 * nv for _, nv in VCHUNKS]
    yb, tb, wg = pl.pallas_call(
        functools.partial(first_kernel, nlat),
        out_shape=[
            jax.ShapeDtypeStruct((ORDERS_PER, npts, 2 * CH), BF16),
            jax.ShapeDtypeStruct((ORDERS_PER, DEGREES, npts), BF16),
            jax.ShapeDtypeStruct((NVAR, CH), F32),
        ],
        in_specs=[any_spec] * 3 + [vmem] * 2 + [any_spec] * 2 + [vmem] + [any_spec],
        out_specs=[any_spec] * 2 + [vmem],
        scratch_shapes=[
            pltpu.VMEM((ROWS, NLON, CH), BF16),
            pltpu.VMEM((NVAR, ROWS, NLON), BF16),
            pltpu.VMEM((NVAR, ROWS, NLON), BF16),
            pltpu.VMEM((nlat * MPAD, LPAD), BF16),
            pltpu.VMEM((8, 128), F32),
            pltpu.VMEM((16, npts), F32),
            pltpu.VMEM((NTILE, 4 * NVAR, 128), F32),
            pltpu.VMEM((NTILE, 4 * NVAR, 128), F32),
            pltpu.VMEM((4 * NVAR, LPAD), F32),
            pltpu.VMEM((4 * NVAR, LPAD), BF16),
        ]
        + [pltpu.VMEM((ENS, n, LBLK), BF16) for n in chunk_rows] * 2
        + [
            pltpu.VMEM((4 * NVAR, LPAD), BF16),
            pltpu.VMEM((nlat, MPAD, 128), BF16),
            pltpu.VMEM((nlat, MPAD, 128), BF16),
            pltpu.VMEM((nlat, 8, 128), BF16),
            pltpu.VMEM((nlat, MPAD, 128), BF16),
            pltpu.VMEM((nlat, MPAD, 128), BF16),
            pltpu.VMEM((nlat, 8, 128), BF16),
            pltpu.VMEM((nlat * MPAD, 128), F32),
            pltpu.VMEM((nlat * 8, 128), F32),
            pltpu.VMEM((2 * NVAR, LBLK), F32),
            pltpu.VMEM((2 * NVAR, 128), F32),
            pltpu.VMEM((NVAR, CH), F32),
            pltpu.VMEM((5, max(piece, 8), CH), F32),
            pltpu.VMEM((nz, piece, CH), F32),
            pltpu.VMEM((n4, piece, CH), F32),
            pltpu.VMEM((ENS, piece, CH), F32),
            pltpu.VMEM((nz, piece, CH), F32),
            pltpu.VMEM((nz, 8, CH), F32),
            pltpu.VMEM((n4, 8, CH), F32),
            pltpu.VMEM((ENS, 8, CH), F32),
            pltpu.VMEM((DEGREES * 16, npts), F32),
            pltpu.VMEM((ORDERS_PER, DEGREES, npts), BF16),
            pltpu.VMEM((2, nlat * MPAD, 128), F32),
            pltpu.VMEM((nlat * 8, 128), F32),
            pltpu.VMEM((256, ROWS * CH), BF16),
            pltpu.VMEM((128, ROWS * CH), F32),
            pltpu.VMEM((128, ROWS * CH), BF16),
            pltpu.VMEM((nlat * MP, 256), BF16),
            pltpu.VMEM((nlat * 6, 128), F32),
            pltpu.VMEM((ORDERS_PER, npts, 2 * CH), BF16),
            dma((9,)), dma((3,)), dma((3,)), dma((3,)), dma((3,)), dma((3,)), dma((3,)),
            dma((7,)), dma((7,)), dma((2,)),
        ],
        compiler_params=pltpu.CompilerParams(
            collective_id=0, has_side_effects=True, vmem_limit_bytes=62 * 1024 * 1024
        ),
        name="loss_and_transform",
    )(features, previous, target, wt, var_weight.reshape(1, NVAR),
      jnp.asarray(basis), jnp.asarray(area), jnp.asarray(cosine), jnp.asarray(diag))

    spectral, wg = pl.pallas_call(
        second_kernel,
        out_shape=[
            jax.ShapeDtypeStruct((1, ORDERS_PER, DEGREES, 2, CH), BF16),
            jax.ShapeDtypeStruct((NVAR, CH), F32),
        ],
        in_specs=[any_spec] * 3,
        out_specs=[any_spec] * 2,
        scratch_shapes=[
            pltpu.VMEM((ORDERS_PER, DEGREES, npts), BF16),
            pltpu.VMEM((ORDERS_PER, npts, 2 * CH), BF16),
            pltpu.VMEM((ORDERS_PER, DEGREES, 2, CH), BF16),
            pltpu.VMEM((2, 2, 2 * DEGREES, 128), F32),
            dma((ORDERS_PER,)), dma((ORDERS_PER,)), dma((ORDERS_PER,)), dma,
        ],
        compiler_params=pltpu.CompilerParams(vmem_limit_bytes=62 * 1024 * 1024),
        name="latitude_transform",
    )(tb, yb, wg)
    return spectral, wg.T


def solution(mesh):
    placed = (
        P("ens", "lat", None, None),
        P("ens", None, "lat", None),
        P(None, "lat", None),
        P(),
        P(),
    )
    return jax.shard_map(
        functools.partial(local, mesh.shape["lat"]),
        mesh=mesh,
        in_specs=placed,
        out_specs=(P("ens", "lat", None, None, None), P()),
        check_vma=False,
    )
```

```python
import functools
import math

import jax
import jax.numpy as jnp
import ml_dtypes
import numpy as np
from jax import lax
from jax.experimental import pallas as pl
from jax.experimental.pallas import tpu as pltpu
from jax.sharding import PartitionSpec as P

FULL_LAT = 721
DEGREES = 352
ORDERS_PER = 11
MP = 2 * ORDERS_PER
MPAD = 24
ENS = 8
ROWS = 4
NLON = 1440
LPAD = 1536
LBLK = 384
NTILE = LPAD // 128
CH = 256
NVAR = 72
OCTETS = NVAR // 8
VCHUNKS = ((0, 32), (32, 32), (64, 8))

smoothing = 0.1
loss_scale = 2048.0
F32 = jnp.float32
BF16 = jnp.bfloat16
MESH = pl.DeviceIdType.MESH


@functools.lru_cache(maxsize=None)
def tables(lat_count):
    rows = ROWS * lat_count
    first = (FULL_LAT - rows) // 2
    colat = np.pi * (np.arange(rows) + first) / (FULL_LAT - 1)
    total = NLON * np.sum(np.sin(np.pi * np.arange(FULL_LAT) / (FULL_LAT - 1)))
    area = np.zeros((lat_count, 8, 128), np.float32)
    area[:, :ROWS] = (loss_scale * np.sin(colat) / total).reshape(lat_count, ROWS, 1)
    order_of = (np.arange(lat_count)[None, :] * ROWS + np.arange(ROWS)[:, None]).reshape(-1)
    theta = colat[order_of]
    cosine = np.broadcast_to(np.cos(theta), (16, rows)).astype(np.float32)
    count = ORDERS_PER * lat_count
    lg = np.array([math.lgamma(m + 1.5) - math.lgamma(m + 1.0) - math.lgamma(1.5) for m in range(count)])
    diag = np.exp(0.5 * lg[:, None] + np.arange(count)[:, None] * np.log(np.sin(theta))[None, :])
    diag = diag * math.sqrt(0.25 / math.pi)
    diag_table = np.zeros((lat_count, 16, rows), np.float32)
    diag_table[:, :ORDERS_PER] = diag.reshape(lat_count, ORDERS_PER, rows)
    m = np.arange(count)
    j = np.arange(NLON)
    angle = 2.0 * np.pi / NLON * ((m[:, None] * j[None, :]) % NLON)
    ow = np.where(m == 0, 1.0, 2.0)[:, None]
    basis = np.zeros((lat_count, MPAD, LPAD))
    basis[:, 0:MP:2, :NLON] = (ow * np.cos(angle)).reshape(lat_count, ORDERS_PER, NLON)
    basis[:, 1:MP:2, :NLON] = (-ow * np.sin(angle)).reshape(lat_count, ORDERS_PER, NLON)
    basis = basis.reshape(lat_count * MPAD, LPAD).astype(ml_dtypes.bfloat16)
    return area, cosine, diag_table, basis


def softened_slope(delta):
    return delta * lax.rsqrt(delta * delta + smoothing * smoothing)


def nt_dot(a, b):
    return lax.dot_general(a, b, (((1,), (1,)), ((), ())), preferred_element_type=F32)


def first_kernel(
    nlat,
    feat, prev, tgt, wt, vw, basis, area, cosx, diag,
    spec, wg,
    featv, prevv, tgtv, basisv, areav, diagv, prev2, tgt2, fc, fsend,
    fr0, fr1, fr2, bs0, bs1, bs2, grad, ss0, ss1, ss2, rv0, rv1, rv2, s2f, m2f,
    tgo, sco, wgp, wsum, wa, wb, wfin, tleg, t2f, t2b,
    x01, x2f, bd01, bd2f, bd2, lhs01, lhs2, ybuf, ov,
    in_sem, f_send, f_recv, b_send, b_recv, l_send, l_recv, w_send, w_recv, wc_recv, out_sem,
):
    me_e = lax.axis_index("ens")
    me_q = lax.axis_index("lat")
    npts = ROWS * nlat
    nz = nlat // 4
    me_z, me_y, me_c = me_q // 4, lax.rem(me_q, 4) // 2, lax.rem(me_q, 2)
    zc_count, ey_count = 2 * nz, 2 * ENS
    me_zc, me_ey = me_z * 2 + me_c, me_e * 2 + me_y
    frecv = (fr0, fr1, fr2)
    bsend = (bs0, bs1, bs2)
    ssend = (ss0, ss1, ss2)
    rout = (rv0, rv1, rv2)

    loads = [pltpu.make_async_copy(feat.at[0, r], featv.at[r], in_sem.at[r]) for r in range(ROWS)]
    loads.append(pltpu.make_async_copy(prev.at[0], prevv, in_sem.at[4]))
    loads.append(pltpu.make_async_copy(tgt, tgtv, in_sem.at[5]))
    loads.append(pltpu.make_async_copy(area.at[me_q], areav, in_sem.at[6]))
    loads.append(pltpu.make_async_copy(diag.at[me_q], diagv, in_sem.at[7]))
    loads.append(pltpu.make_async_copy(basis, basisv, in_sem.at[8]))
    for i in (4, 0, 1, 2, 3, 5, 6, 7, 8):
        loads[i].start()

    barrier = pltpu.get_barrier_semaphore()

    def ey_device(ens, y):
        return {"ens": ens, "lat": me_z * 4 + y * 2 + me_c}

    def zc_device(i):
        return {"lat": (i // 2) * 4 + me_y * 2 + lax.rem(i, 2)}

    def greet_ens(s, c):
        pl.semaphore_signal(barrier, inc=1, device_id={"ens": lax.rem(me_e + s, ENS)}, device_id_type=MESH)
        return c

    def greet_lat(s, c):
        pl.semaphore_signal(barrier, inc=1, device_id={"lat": lax.rem(me_q + s, nlat)}, device_id_type=MESH)
        return c

    lax.fori_loop(1, ENS, greet_ens, 0)
    lax.fori_loop(1, nlat, greet_lat, 0)

    def greet_ey(s, c):
        pl.semaphore_signal(
            barrier, inc=1, device_id=ey_device(lax.rem(me_e + s, ENS), 1 - me_y), device_id_type=MESH
        )
        return c

    lax.fori_loop(1, ENS, greet_ey, 0)

    fc[:, LPAD - 128 : LPAD] = jnp.zeros((4 * NVAR, 128), F32)
    prev2[NTILE - 1] = jnp.zeros((4 * NVAR, 128), F32)
    loads[4].wait()

    def widen_prev(i, c):
        pair = jnp.concatenate([prevv[2 * i].astype(F32), prevv[2 * i + 1].astype(F32)], axis=0)
        for lt in range(NTILE):
            wide = min(128, NLON - 128 * lt)
            prev2[lt, pl.ds(pl.multiple_of(8 * i, 8), 8), 0:wide] = pair[:, 128 * lt : 128 * lt + wide]
        return c

    lax.fori_loop(0, NVAR // 2, widen_prev, 0)
    for r in range(ROWS):
        loads[r].wait()
        fc[NVAR * r : NVAR * (r + 1), 0:NLON] = nt_dot(wt[...], featv[r])

    pl.semaphore_wait(barrier, ENS - 1 + nlat - 1 + ENS - 1)

    my_blk = me_e // 2
    my_half = lax.rem(me_e, 2)
    for k, (v0, nv) in enumerate(VCHUNKS):
        base, nh = 4 * v0, 2 * nv
        for lt in range(NTILE):
            lanes = slice(128 * lt, 128 * lt + 128)
            parts = []
            for r in range(ROWS):
                field = fc[NVAR * r + v0 : NVAR * r + v0 + nv, lanes] + prev2[lt, pl.ds(4 * v0 + r, nv, stride=4), :]
                parts.append(field * field * field * jnp.abs(field))
            fsend[base : base + 4 * nv, lanes] = jnp.concatenate(parts, axis=0).astype(BF16)

        def block_of(dev, base=base, nh=nh):
            row = pl.multiple_of(base + lax.rem(dev, 2) * nh, 16)
            lane = pl.multiple_of((dev // 2) * LBLK, 128)
            return pl.ds(row, nh), pl.ds(lane, LBLK)

        def send_fwd(s, c, k=k, block_of=block_of):
            dev = lax.rem(me_e + s, ENS)
            rows, lanes = block_of(dev)
            pltpu.make_async_remote_copy(
                src_ref=fsend.at[rows, lanes],
                dst_ref=frecv[k].at[me_e],
                send_sem=f_send.at[k],
                recv_sem=f_recv.at[k],
                device_id={"ens": dev},
                device_id_type=MESH,
            ).start()
            return c

        lax.fori_loop(1, ENS, send_fwd, 0)
        rows, lanes = block_of(me_e)
        pltpu.make_async_copy(fsend.at[rows, lanes], frecv[k].at[me_e], f_recv.at[k]).start()

    loads[5].wait()
    tgt2[NTILE - 1] = jnp.zeros((4 * NVAR, 128), F32)

    def widen_tgt(i, c):
        pair = jnp.concatenate([tgtv[2 * i].astype(F32), tgtv[2 * i + 1].astype(F32)], axis=0)
        for lt in range(NTILE):
            wide = min(128, NLON - 128 * lt)
            tgt2[lt, pl.ds(pl.multiple_of(8 * i, 8), 8), 0:wide] = pair[:, 128 * lt : 128 * lt + wide]
        return c

    lax.fori_loop(0, NVAR // 2, widen_tgt, 0)
    loads[6].wait()
    lane_id = lax.broadcasted_iota(jnp.int32, (NVAR, NVAR), 1)
    row_id = lax.broadcasted_iota(jnp.int32, (NVAR, NVAR), 0)
    vcol = jnp.sum(jnp.where(lane_id == row_id, vw[...], 0.0), axis=1, keepdims=True)
    my_lane = pl.multiple_of(my_blk * LBLK, 128)
    for k, (v0, nv) in enumerate(VCHUNKS):
        for rr in range(2):
            r = 2 * my_half + rr
            at = 2 * v0 + rr * nv
            for i in range(3):
                tgo[at : at + nv, 128 * i : 128 * i + 128] = tgt2[3 * my_blk + i, pl.ds(4 * v0 + r, nv, stride=4), :]
            sco[at : at + nv, :] = vcol[v0 : v0 + nv] * areav[pl.ds(r, 1), :]

    loads[7].wait()
    order = (lax.broadcasted_iota(jnp.int32, (16, npts), 0) + ORDERS_PER * me_q).astype(F32)
    order_sq = order * order

    def legendre_step(l, carry):
        last, before, eps = carry
        lf = jnp.zeros((16, npts), F32) + l.astype(F32)
        lsq = lf * lf
        gap = lsq - order_sq
        ratio = jnp.maximum(gap, 1.0) / jnp.maximum(4.0 * lsq - 1.0, 1.0)
        inv = lax.rsqrt(ratio)
        new = inv * (cosx[...] * last - eps * before)
        new = jnp.where(lf == order, diagv[...], jnp.where(lf > order, new, 0.0))
        tleg[pl.ds(pl.multiple_of(16 * l, 16), 16), :] = new
        return new, last, jnp.where(gap > 0.0, ratio * inv, 0.0)

    zero = diagv[...] * 0.0
    lax.fori_loop(0, DEGREES, legendre_step, (zero, zero, zero))

    for k, (v0, nv) in enumerate(VCHUNKS):
        base, nh = 4 * v0, 2 * nv
        pltpu.make_async_copy(frecv[k], frecv[k], f_recv.at[k]).wait()

        def loss_tile(i, c, k=k, v0=v0):
            row = pl.multiple_of((i // 3) * 16, 16)
            lane = pl.multiple_of(lax.rem(i, 3) * 128, 128)
            fields = []
            for e in range(ENS):
                u = frecv[k][e, pl.ds(row, 16), pl.ds(lane, 128)].astype(F32)
                mag = lax.rsqrt(lax.rsqrt(jnp.abs(u)))
                fields.append(jnp.where(u < 0.0, -mag, mag))
            pair_sum = [None] * ENS
            for a in range(ENS):
                for b in range(a + 1, ENS):
                    s = softened_slope(fields[a] - fields[b])
                    pair_sum[a] = s if pair_sum[a] is None else pair_sum[a] + s
                    pair_sum[b] = -s if pair_sum[b] is None else pair_sum[b] - s
            at = pl.multiple_of(2 * v0 + row, 16)
            aim = tgo[pl.ds(at, 16), pl.ds(lane, 128)]
            scale = sco[pl.ds(at, 16), :]
            for e in range(ENS):
                g = softened_slope(fields[e] - aim) * (1.0 / ENS) - pair_sum[e] * (1.0 / (ENS * (ENS - 1)))
                bsend[k][e, pl.ds(row, 16), pl.ds(lane, 128)] = (scale * g).astype(BF16)
            return c

        lax.fori_loop(0, (nh // 16) * 3, loss_tile, 0)

        my_rows = pl.ds(pl.multiple_of(base + my_half * nh, 16), nh)
        my_lanes = pl.ds(my_lane, LBLK)

        def send_bwd(s, c, k=k, my_rows=my_rows, my_lanes=my_lanes):
            dev = lax.rem(me_e + s, ENS)
            pltpu.make_async_remote_copy(
                src_ref=bsend[k].at[dev],
                dst_ref=grad.at[my_rows, my_lanes],
                send_sem=b_send.at[k],
                recv_sem=b_recv.at[k],
                device_id={"ens": dev},
                device_id_type=MESH,
            ).start()
            return c

        lax.fori_loop(1, ENS, send_bwd, 0)
        pltpu.make_async_copy(bsend[k].at[me_e], grad.at[my_rows, my_lanes], b_recv.at[k]).start()

    t2f[...] = jnp.zeros(t2f.shape, F32)

    def spread(m, c):
        rows = tleg[pl.ds(m, DEGREES, stride=16), :]
        for p in range(2):
            t2f[p, pl.ds(p, DEGREES, stride=2), :] = rows
            t2b[m, :, npts * p : npts * (p + 1)] = t2f[p].astype(BF16)
        return c

    lax.fori_loop(0, ORDERS_PER, spread, 0)

    bd01[...] = jnp.zeros(bd01.shape, BF16)
    bd2f[...] = jnp.zeros(bd2f.shape, F32)
    tail = wt[64:72, :].astype(F32)
    for r in range(ROWS):
        for k in range(2):
            bd01[128 * k + 32 * r : 128 * k + 32 * r + 32, CH * r : CH * r + CH] = wt[32 * k : 32 * k + 32, :]
        for g in range(4):
            bd2f[32 * g + 8 * r : 32 * g + 8 * r + 8, CH * r : CH * r + CH] = tail
    bd2[...] = bd2f[...].astype(BF16)

    loads[8].wait()
    m2f[...] = jnp.zeros(m2f.shape, F32)
    for k, (v0, nv) in enumerate(VCHUNKS):
        base = 4 * v0
        rows = pl.ds(base, 4 * nv)
        pltpu.make_async_copy(grad.at[rows, :], grad.at[rows, :], b_recv.at[k]).wait()

        total = None
        for r in range(ROWS):
            if nv % 16 == 0:
                g = grad[base + r * nv : base + (r + 1) * nv, 0:NLON]
            else:
                pair = grad[base + (r // 2) * 2 * nv : base + (r // 2 + 1) * 2 * nv, 0:NLON]
                g = pair.astype(F32)[(r % 2) * nv : (r % 2 + 1) * nv].astype(BF16)
            term = jnp.dot(g, featv[r], preferred_element_type=F32)
            total = term if total is None else total + term
        wgp[v0 : v0 + nv, :] = total
        if k == 2:
            for o in range(OCTETS):
                rows_o = wgp.at[pl.ds(8 * o, 8)]

                @pl.when(me_ey == o)
                def _(rows_o=rows_o):
                    pltpu.make_async_copy(rows_o, wa.at[me_ey], w_recv.at[0]).start()

                @pl.when(me_ey != o)
                def _(rows_o=rows_o, o=o):
                    pltpu.make_async_remote_copy(
                        src_ref=rows_o,
                        dst_ref=wa.at[me_ey],
                        send_sem=w_send.at[o],
                        recv_sem=w_recv.at[0],
                        device_id=ey_device(jnp.int32(o // 2), jnp.int32(o % 2)),
                        device_id_type=MESH,
                    ).start()

        waves = nt_dot(basisv[...], grad[rows, :])
        if k < 2:
            ssend[k][...] = waves.reshape(nlat, MPAD, 128).astype(BF16)
        else:
            s2f[:, 0:32] = waves
            for j in range(6):
                cols = [s2f[pl.ds(6 * g + j, nlat, stride=MPAD), :][:, 0:32] for g in range(4)]
                m2f[pl.ds(j, nlat, stride=8), :] = jnp.concatenate(cols, axis=1)
            ssend[k][...] = m2f[...].reshape(nlat, 8, 128).astype(BF16)

        def send_lat(s, c, k=k):
            dev = lax.rem(me_q + s, nlat)
            pltpu.make_async_remote_copy(
                src_ref=ssend[k].at[dev],
                dst_ref=rout[k].at[me_q],
                send_sem=l_send.at[k],
                recv_sem=l_recv.at[k],
                device_id={"lat": dev},
                device_id_type=MESH,
            ).start()
            return c

        lax.fori_loop(1, nlat, send_lat, 0)
        pltpu.make_async_copy(ssend[k].at[me_q], rout[k].at[me_q], l_recv.at[k]).start()

    def gather(k):
        pltpu.make_async_copy(rout[k], rout[k], l_recv.at[k]).wait()
        if k == 2:
            x2f[...] = rout[k][...].astype(F32).reshape(nlat * 8, 128)
            for j in range(6):
                lhs2[nlat * j : nlat * (j + 1), :] = x2f[pl.ds(j, nlat, stride=8), :]
        else:
            x01[k] = rout[k][...].astype(F32).reshape(nlat * MPAD, 128)
            for i in range(MP):
                lhs01[nlat * i : nlat * (i + 1), 128 * k : 128 * k + 128] = x01[k, pl.ds(i, nlat, stride=MPAD), :].astype(BF16)

    gather(0)

    @pl.when(me_ey < OCTETS)
    def _():
        pltpu.make_async_copy(wa, wa, w_recv.at[0]).wait()
        wsum[0] = jnp.sum(wa[...], axis=0)

        def send_zc(s, c):
            pltpu.make_async_remote_copy(
                src_ref=wsum.at[0],
                dst_ref=wb.at[me_zc],
                send_sem=w_send.at[OCTETS],
                recv_sem=w_recv.at[1],
                device_id=zc_device(lax.rem(me_zc + s, zc_count)),
                device_id_type=MESH,
            ).start()
            return c

        lax.fori_loop(1, zc_count, send_zc, 0)
        pltpu.make_async_copy(wsum.at[0], wb.at[me_zc], w_recv.at[1]).start()

    gather(1)
    gather(2)
    for g in range(4):
        nj = min(6, MP - 6 * g)
        n = nj * nlat
        group = lax.broadcasted_iota(jnp.int32, (n, 128), 1) // 32
        last = jnp.where(group == g, lhs2[0:n, :], 0.0).astype(BF16)
        y = jnp.dot(lhs01[6 * g * nlat : 6 * g * nlat + n, :], bd01[...], preferred_element_type=F32)
        y = y + jnp.dot(last, bd2[...], preferred_element_type=F32)
        for j in range(nj):
            m, p = (6 * g + j) // 2, (6 * g + j) % 2
            for r in range(ROWS):
                at = (p * ROWS + r) * nlat
                ybuf[m, at : at + nlat, :] = y[j * nlat : (j + 1) * nlat, CH * r : CH * r + CH].astype(BF16)

    @pl.when(me_ey < OCTETS)
    def _():
        pltpu.make_async_copy(wb, wb, w_recv.at[1]).wait()
        wsum[1] = jnp.sum(wb[...], axis=0)

        def send_ey(s, c):
            i = lax.rem(me_ey + s, ey_count)
            pltpu.make_async_remote_copy(
                src_ref=wsum.at[1],
                dst_ref=wfin.at[me_ey],
                send_sem=w_send.at[OCTETS + 1],
                recv_sem=wc_recv,
                device_id=ey_device(i // 2, lax.rem(i, 2)),
                device_id_type=MESH,
            ).start()
            return c

        lax.fori_loop(1, ey_count, send_ey, 0)
        pltpu.make_async_copy(wsum.at[1], wfin.at[me_ey], wc_recv).start()

    for m in range(ORDERS_PER):
        res = jnp.dot(t2b[m], ybuf[m], preferred_element_type=F32).astype(BF16)
        ov[m] = res.reshape(DEGREES, 2, CH)
        pltpu.make_async_copy(ov.at[m], spec.at[0, m], out_sem.at[m]).start()

    pltpu.make_async_copy(wfin, wfin, wc_recv).wait()
    wg[...] = wfin[...].reshape(NVAR, CH)

    for k in range(3):
        part = frecv[k].at[pl.ds(0, ENS - 1)]
        pltpu.make_async_copy(part, part, f_send.at[k]).wait()
        part = bsend[k].at[pl.ds(0, ENS - 1)]
        pltpu.make_async_copy(part, part, b_send.at[k]).wait()
        part = ssend[k].at[pl.ds(0, nlat - 1)]
        pltpu.make_async_copy(part, part, l_send.at[k]).wait()
    for o in range(OCTETS):

        @pl.when(me_ey != o)
        def _(o=o):
            rows_o = wgp.at[pl.ds(8 * o, 8)]
            pltpu.make_async_copy(rows_o, rows_o, w_send.at[o]).wait()

    @pl.when(me_ey < OCTETS)
    def _():
        part = wb.at[pl.ds(0, zc_count - 1)]
        pltpu.make_async_copy(part, part, w_send.at[OCTETS]).wait()
        part = wa.at[pl.ds(0, ey_count - 1)]
        pltpu.make_async_copy(part, part, w_send.at[OCTETS + 1]).wait()

    for m in range(ORDERS_PER):
        pltpu.make_async_copy(ov.at[m], spec.at[0, m], out_sem.at[m]).wait()


def second_kernel(spec, wg, out, wg_out, held, in_sem, out_sem, w_sem):
    passed = pltpu.make_async_copy(wg, wg_out, w_sem)
    passed.start()
    for m in range(ORDERS_PER):
        pltpu.make_async_copy(spec.at[0, m], held.at[m], in_sem.at[m]).start()
    for m in range(ORDERS_PER):
        pltpu.make_async_copy(spec.at[0, m], held.at[m], in_sem.at[m]).wait()
        pltpu.make_async_copy(held.at[m], out.at[0, m], out_sem.at[m]).start()
    for m in range(ORDERS_PER):
        pltpu.make_async_copy(held.at[m], out.at[0, m], out_sem.at[m]).wait()
    passed.wait()


def local(nlat, features, previous, target, weight, var_weight):
    area, cosine, diag, basis = tables(nlat)
    npts = ROWS * nlat
    nz = nlat // 4
    any_spec = pl.BlockSpec(memory_space=pl.ANY)
    vmem = pl.BlockSpec(memory_space=pltpu.VMEM)
    wt = weight.T
    dma = pltpu.SemaphoreType.DMA
    chunk_rows = [2 * nv for _, nv in VCHUNKS]
    spec, wg = pl.pallas_call(
        functools.partial(first_kernel, nlat),
        out_shape=[
            jax.ShapeDtypeStruct((1, ORDERS_PER, DEGREES, 2, CH), BF16),
            jax.ShapeDtypeStruct((NVAR, CH), F32),
        ],
        in_specs=[any_spec] * 3 + [vmem] * 2 + [any_spec] * 2 + [vmem] + [any_spec],
        out_specs=[any_spec, vmem],
        scratch_shapes=[
            pltpu.VMEM((ROWS, NLON, CH), BF16),
            pltpu.VMEM((NVAR, ROWS, NLON), BF16),
            pltpu.VMEM((NVAR, ROWS, NLON), BF16),
            pltpu.VMEM((nlat * MPAD, LPAD), BF16),
            pltpu.VMEM((8, 128), F32),
            pltpu.VMEM((16, npts), F32),
            pltpu.VMEM((NTILE, 4 * NVAR, 128), F32),
            pltpu.VMEM((NTILE, 4 * NVAR, 128), F32),
            pltpu.VMEM((4 * NVAR, LPAD), F32),
            pltpu.VMEM((4 * NVAR, LPAD), BF16),
        ]
        + [pltpu.VMEM((ENS, n, LBLK), BF16) for n in chunk_rows] * 2
        + [
            pltpu.VMEM((4 * NVAR, LPAD), BF16),
            pltpu.VMEM((nlat, MPAD, 128), BF16),
            pltpu.VMEM((nlat, MPAD, 128), BF16),
            pltpu.VMEM((nlat, 8, 128), BF16),
            pltpu.VMEM((nlat, MPAD, 128), BF16),
            pltpu.VMEM((nlat, MPAD, 128), BF16),
            pltpu.VMEM((nlat, 8, 128), BF16),
            pltpu.VMEM((nlat * MPAD, 128), F32),
            pltpu.VMEM((nlat * 8, 128), F32),
            pltpu.VMEM((2 * NVAR, LBLK), F32),
            pltpu.VMEM((2 * NVAR, 128), F32),
            pltpu.VMEM((NVAR, CH), F32),
            pltpu.VMEM((2, 8, CH), F32),
            pltpu.VMEM((2 * ENS, 8, CH), F32),
            pltpu.VMEM((2 * nz, 8, CH), F32),
            pltpu.VMEM((OCTETS, 8, CH), F32),
            pltpu.VMEM((DEGREES * 16, npts), F32),
            pltpu.VMEM((2, 2 * DEGREES, npts), F32),
            pltpu.VMEM((ORDERS_PER, 2 * DEGREES, 2 * npts), BF16),
            pltpu.VMEM((2, nlat * MPAD, 128), F32),
            pltpu.VMEM((nlat * 8, 128), F32),
            pltpu.VMEM((256, ROWS * CH), BF16),
            pltpu.VMEM((128, ROWS * CH), F32),
            pltpu.VMEM((128, ROWS * CH), BF16),
            pltpu.VMEM((nlat * MP, 256), BF16),
            pltpu.VMEM((nlat * 6, 128), F32),
            pltpu.VMEM((ORDERS_PER, 2 * npts, CH), BF16),
            pltpu.VMEM((ORDERS_PER, DEGREES, 2, CH), BF16),
            dma((9,)), dma((3,)), dma((3,)), dma((3,)), dma((3,)), dma((3,)), dma((3,)),
            dma((OCTETS + 2,)), dma((2,)), dma, dma((ORDERS_PER,)),
        ],
        compiler_params=pltpu.CompilerParams(
            collective_id=0, has_side_effects=True, vmem_limit_bytes=62 * 1024 * 1024
        ),
        name="loss_and_transform",
    )(features, previous, target, wt, var_weight.reshape(1, NVAR),
      jnp.asarray(basis), jnp.asarray(area), jnp.asarray(cosine), jnp.asarray(diag))

    spectral, wg = pl.pallas_call(
        second_kernel,
        out_shape=[
            jax.ShapeDtypeStruct((1, ORDERS_PER, DEGREES, 2, CH), BF16),
            jax.ShapeDtypeStruct((NVAR, CH), F32),
        ],
        in_specs=[any_spec] * 2,
        out_specs=[any_spec] * 2,
        scratch_shapes=[
            pltpu.VMEM((ORDERS_PER, DEGREES, 2, CH), BF16),
            dma((ORDERS_PER,)), dma((ORDERS_PER,)), dma,
        ],
        compiler_params=pltpu.CompilerParams(vmem_limit_bytes=62 * 1024 * 1024),
        name="hand_over",
    )(spec, wg)
    return spectral, wg.T


def solution(mesh):
    placed = (
        P("ens", "lat", None, None),
        P("ens", None, "lat", None),
        P(None, "lat", None),
        P(),
        P(),
    )
    return jax.shard_map(
        functools.partial(local, mesh.shape["lat"]),
        mesh=mesh,
        in_specs=placed,
        out_specs=(P("ens", "lat", None, None, None), P()),
        check_vma=False,
    )
```

```python
import functools
import math

import jax
import jax.numpy as jnp
import ml_dtypes
import numpy as np
from jax import lax
from jax.experimental import pallas as pl
from jax.experimental.pallas import tpu as pltpu
from jax.sharding import PartitionSpec as P

FULL_LAT = 721
DEGREES = 352
ORDERS_PER = 11
MP = 2 * ORDERS_PER
MPAD = 24
ENS = 8
ROWS = 4
NLON = 1440
LPAD = 1536
LBLK = 384
NTILE = LPAD // 128
CH = 256
NVAR = 72
OCTETS = NVAR // 8
VCHUNKS = ((0, 32), (32, 32), (64, 8))

smoothing = 0.1
loss_scale = 2048.0
F32 = jnp.float32
BF16 = jnp.bfloat16
MESH = pl.DeviceIdType.MESH


@functools.lru_cache(maxsize=None)
def tables(lat_count):
    rows = ROWS * lat_count
    first = (FULL_LAT - rows) // 2
    colat = np.pi * (np.arange(rows) + first) / (FULL_LAT - 1)
    total = NLON * np.sum(np.sin(np.pi * np.arange(FULL_LAT) / (FULL_LAT - 1)))
    area = np.zeros((lat_count, 8, 128), np.float32)
    area[:, :ROWS] = (loss_scale * np.sin(colat) / total).reshape(lat_count, ROWS, 1)
    order_of = (np.arange(lat_count)[None, :] * ROWS + np.arange(ROWS)[:, None]).reshape(-1)
    theta = colat[order_of]
    cosine = np.broadcast_to(np.cos(theta), (16, rows)).astype(np.float32)
    count = ORDERS_PER * lat_count
    lg = np.array([math.lgamma(m + 1.5) - math.lgamma(m + 1.0) - math.lgamma(1.5) for m in range(count)])
    diag = np.exp(0.5 * lg[:, None] + np.arange(count)[:, None] * np.log(np.sin(theta))[None, :])
    diag = diag * math.sqrt(0.25 / math.pi)
    diag_table = np.zeros((lat_count, 16, rows), np.float32)
    diag_table[:, :ORDERS_PER] = diag.reshape(lat_count, ORDERS_PER, rows)
    m = np.arange(count)
    j = np.arange(NLON)
    angle = 2.0 * np.pi / NLON * ((m[:, None] * j[None, :]) % NLON)
    ow = np.where(m == 0, 1.0, 2.0)[:, None]
    basis = np.zeros((lat_count, MPAD, LPAD))
    basis[:, 0:MP:2, :NLON] = (ow * np.cos(angle)).reshape(lat_count, ORDERS_PER, NLON)
    basis[:, 1:MP:2, :NLON] = (-ow * np.sin(angle)).reshape(lat_count, ORDERS_PER, NLON)
    basis = basis.reshape(lat_count * MPAD, LPAD).astype(ml_dtypes.bfloat16)
    return area, cosine, diag_table, basis


def softened_slope(delta):
    return delta * lax.rsqrt(delta * delta + smoothing * smoothing)


def nt_dot(a, b):
    return lax.dot_general(a, b, (((1,), (1,)), ((), ())), preferred_element_type=F32)


def first_kernel(
    nlat,
    feat, prev, tgt, wt, vw, basis, area, cosx, diag,
    spec, wg,
    featv, prevv, tgtv, basisv, areav, diagv, prev2, tgt2, fc, fsend,
    fr0, fr1, fr2, bs0, bs1, bs2, grad, ss0, ss1, ss2, rv0, rv1, rv2, s2f, m2f,
    tgo, sco, wgp, wsum, wa, wb, wfin, tleg, t2f, t2b,
    x01, x2f, bd01, bd2f, bd2, lhs01, lhs2, ybuf,
    in_sem, f_send, f_recv, b_send, b_recv, l_send, l_recv, w_send, w_recv, wc_recv,
):
    me_e = lax.axis_index("ens")
    me_q = lax.axis_index("lat")
    npts = ROWS * nlat
    nz = nlat // 4
    me_z, me_y, me_c = me_q // 4, lax.rem(me_q, 4) // 2, lax.rem(me_q, 2)
    zc_count, ey_count = 2 * nz, 2 * ENS
    me_zc, me_ey = me_z * 2 + me_c, me_e * 2 + me_y
    frecv = (fr0, fr1, fr2)
    bsend = (bs0, bs1, bs2)
    ssend = (ss0, ss1, ss2)
    rout = (rv0, rv1, rv2)

    loads = [pltpu.make_async_copy(feat.at[0, r], featv.at[r], in_sem.at[r]) for r in range(ROWS)]
    loads.append(pltpu.make_async_copy(prev.at[0], prevv, in_sem.at[4]))
    loads.append(pltpu.make_async_copy(tgt, tgtv, in_sem.at[5]))
    loads.append(pltpu.make_async_copy(area.at[me_q], areav, in_sem.at[6]))
    loads.append(pltpu.make_async_copy(diag.at[me_q], diagv, in_sem.at[7]))
    loads.append(pltpu.make_async_copy(basis, basisv, in_sem.at[8]))
    for i in (4, 0, 1, 2, 3, 5, 6, 7, 8):
        loads[i].start()

    barrier = pltpu.get_barrier_semaphore()

    def ey_device(ens, y):
        return {"ens": ens, "lat": me_z * 4 + y * 2 + me_c}

    def zc_device(i):
        return {"lat": (i // 2) * 4 + me_y * 2 + lax.rem(i, 2)}

    def greet_ens(s, c):
        pl.semaphore_signal(barrier, inc=1, device_id={"ens": lax.rem(me_e + s, ENS)}, device_id_type=MESH)
        return c

    def greet_lat(s, c):
        pl.semaphore_signal(barrier, inc=1, device_id={"lat": lax.rem(me_q + s, nlat)}, device_id_type=MESH)
        return c

    lax.fori_loop(1, ENS, greet_ens, 0)
    lax.fori_loop(1, nlat, greet_lat, 0)

    def greet_ey(s, c):
        pl.semaphore_signal(
            barrier, inc=1, device_id=ey_device(lax.rem(me_e + s, ENS), 1 - me_y), device_id_type=MESH
        )
        return c

    lax.fori_loop(1, ENS, greet_ey, 0)

    fc[:, LPAD - 128 : LPAD] = jnp.zeros((4 * NVAR, 128), F32)
    prev2[NTILE - 1] = jnp.zeros((4 * NVAR, 128), F32)
    loads[4].wait()

    def widen_prev(i, c):
        pair = jnp.concatenate([prevv[2 * i].astype(F32), prevv[2 * i + 1].astype(F32)], axis=0)
        for lt in range(NTILE):
            wide = min(128, NLON - 128 * lt)
            prev2[lt, pl.ds(pl.multiple_of(8 * i, 8), 8), 0:wide] = pair[:, 128 * lt : 128 * lt + wide]
        return c

    lax.fori_loop(0, NVAR // 2, widen_prev, 0)
    for r in range(ROWS):
        loads[r].wait()
        fc[NVAR * r : NVAR * (r + 1), 0:NLON] = nt_dot(wt[...], featv[r])

    pl.semaphore_wait(barrier, ENS - 1 + nlat - 1 + ENS - 1)

    my_blk = me_e // 2
    my_half = lax.rem(me_e, 2)
    for k, (v0, nv) in enumerate(VCHUNKS):
        base, nh = 4 * v0, 2 * nv
        for lt in range(NTILE):
            lanes = slice(128 * lt, 128 * lt + 128)
            parts = []
            for r in range(ROWS):
                field = fc[NVAR * r + v0 : NVAR * r + v0 + nv, lanes] + prev2[lt, pl.ds(4 * v0 + r, nv, stride=4), :]
                parts.append(field * field * field * jnp.abs(field))
            fsend[base : base + 4 * nv, lanes] = jnp.concatenate(parts, axis=0).astype(BF16)

        def block_of(dev, base=base, nh=nh):
            row = pl.multiple_of(base + lax.rem(dev, 2) * nh, 16)
            lane = pl.multiple_of((dev // 2) * LBLK, 128)
            return pl.ds(row, nh), pl.ds(lane, LBLK)

        def send_fwd(s, c, k=k, block_of=block_of):
            dev = lax.rem(me_e + s, ENS)
            rows, lanes = block_of(dev)
            pltpu.make_async_remote_copy(
                src_ref=fsend.at[rows, lanes],
                dst_ref=frecv[k].at[me_e],
                send_sem=f_send.at[k],
                recv_sem=f_recv.at[k],
                device_id={"ens": dev},
                device_id_type=MESH,
            ).start()
            return c

        lax.fori_loop(1, ENS, send_fwd, 0)
        rows, lanes = block_of(me_e)
        pltpu.make_async_copy(fsend.at[rows, lanes], frecv[k].at[me_e], f_recv.at[k]).start()

    loads[5].wait()
    tgt2[NTILE - 1] = jnp.zeros((4 * NVAR, 128), F32)

    def widen_tgt(i, c):
        pair = jnp.concatenate([tgtv[2 * i].astype(F32), tgtv[2 * i + 1].astype(F32)], axis=0)
        for lt in range(NTILE):
            wide = min(128, NLON - 128 * lt)
            tgt2[lt, pl.ds(pl.multiple_of(8 * i, 8), 8), 0:wide] = pair[:, 128 * lt : 128 * lt + wide]
        return c

    lax.fori_loop(0, NVAR // 2, widen_tgt, 0)
    loads[6].wait()
    lane_id = lax.broadcasted_iota(jnp.int32, (NVAR, NVAR), 1)
    row_id = lax.broadcasted_iota(jnp.int32, (NVAR, NVAR), 0)
    vcol = jnp.sum(jnp.where(lane_id == row_id, vw[...], 0.0), axis=1, keepdims=True)
    my_lane = pl.multiple_of(my_blk * LBLK, 128)
    for k, (v0, nv) in enumerate(VCHUNKS):
        for rr in range(2):
            r = 2 * my_half + rr
            at = 2 * v0 + rr * nv
            for i in range(3):
                tgo[at : at + nv, 128 * i : 128 * i + 128] = tgt2[3 * my_blk + i, pl.ds(4 * v0 + r, nv, stride=4), :]
            sco[at : at + nv, :] = vcol[v0 : v0 + nv] * areav[pl.ds(r, 1), :]

    loads[7].wait()
    order = (lax.broadcasted_iota(jnp.int32, (16, npts), 0) + ORDERS_PER * me_q).astype(F32)
    order_sq = order * order

    def legendre_step(l, carry):
        last, before, eps = carry
        lf = jnp.zeros((16, npts), F32) + l.astype(F32)
        lsq = lf * lf
        gap = lsq - order_sq
        ratio = jnp.maximum(gap, 1.0) / jnp.maximum(4.0 * lsq - 1.0, 1.0)
        inv = lax.rsqrt(ratio)
        new = inv * (cosx[...] * last - eps * before)
        new = jnp.where(lf == order, diagv[...], jnp.where(lf > order, new, 0.0))
        tleg[pl.ds(pl.multiple_of(16 * l, 16), 16), :] = new
        return new, last, jnp.where(gap > 0.0, ratio * inv, 0.0)

    zero = diagv[...] * 0.0
    state = lax.fori_loop(0, DEGREES // 2, legendre_step, (zero, zero, zero), unroll=8)

    for k, (v0, nv) in enumerate(VCHUNKS):
        base, nh = 4 * v0, 2 * nv
        pltpu.make_async_copy(frecv[k], frecv[k], f_recv.at[k]).wait()

        def loss_tile(i, c, k=k, v0=v0):
            row = pl.multiple_of((i // 3) * 16, 16)
            lane = pl.multiple_of(lax.rem(i, 3) * 128, 128)
            fields = []
            for e in range(ENS):
                u = frecv[k][e, pl.ds(row, 16), pl.ds(lane, 128)].astype(F32)
                mag = lax.rsqrt(lax.rsqrt(jnp.abs(u)))
                fields.append(jnp.where(u < 0.0, -mag, mag))
            pair_sum = [None] * ENS
            for a in range(ENS):
                for b in range(a + 1, ENS):
                    s = softened_slope(fields[a] - fields[b])
                    pair_sum[a] = s if pair_sum[a] is None else pair_sum[a] + s
                    pair_sum[b] = -s if pair_sum[b] is None else pair_sum[b] - s
            at = pl.multiple_of(2 * v0 + row, 16)
            aim = tgo[pl.ds(at, 16), pl.ds(lane, 128)]
            scale = sco[pl.ds(at, 16), :]
            for e in range(ENS):
                g = softened_slope(fields[e] - aim) * (1.0 / ENS) - pair_sum[e] * (1.0 / (ENS * (ENS - 1)))
                bsend[k][e, pl.ds(row, 16), pl.ds(lane, 128)] = (scale * g).astype(BF16)
            return c

        lax.fori_loop(0, (nh // 16) * 3, loss_tile, 0)

        my_rows = pl.ds(pl.multiple_of(base + my_half * nh, 16), nh)
        my_lanes = pl.ds(my_lane, LBLK)

        def send_bwd(s, c, k=k, my_rows=my_rows, my_lanes=my_lanes):
            dev = lax.rem(me_e + s, ENS)
            pltpu.make_async_remote_copy(
                src_ref=bsend[k].at[dev],
                dst_ref=grad.at[my_rows, my_lanes],
                send_sem=b_send.at[k],
                recv_sem=b_recv.at[k],
                device_id={"ens": dev},
                device_id_type=MESH,
            ).start()
            return c

        lax.fori_loop(1, ENS, send_bwd, 0)
        pltpu.make_async_copy(bsend[k].at[me_e], grad.at[my_rows, my_lanes], b_recv.at[k]).start()
        if k == 0:
            lax.fori_loop(DEGREES // 2, DEGREES, legendre_step, state, unroll=8)

    t2f[...] = jnp.zeros(t2f.shape, F32)

    def spread(m, c):
        rows = tleg[pl.ds(m, DEGREES, stride=16), :]
        for p in range(2):
            t2f[p, pl.ds(p, DEGREES, stride=2), :] = rows
            t2b[m, :, npts * p : npts * (p + 1)] = t2f[p].astype(BF16)
        return c

    lax.fori_loop(0, ORDERS_PER, spread, 0)

    bd01[...] = jnp.zeros(bd01.shape, BF16)
    bd2f[...] = jnp.zeros(bd2f.shape, F32)
    tail = wt[64:72, :].astype(F32)
    for r in range(ROWS):
        for k in range(2):
            bd01[128 * k + 32 * r : 128 * k + 32 * r + 32, CH * r : CH * r + CH] = wt[32 * k : 32 * k + 32, :]
        for g in range(4):
            bd2f[32 * g + 8 * r : 32 * g + 8 * r + 8, CH * r : CH * r + CH] = tail
    bd2[...] = bd2f[...].astype(BF16)

    loads[8].wait()
    m2f[...] = jnp.zeros(m2f.shape, F32)
    for k, (v0, nv) in enumerate(VCHUNKS):
        base = 4 * v0
        rows = pl.ds(base, 4 * nv)
        pltpu.make_async_copy(grad.at[rows, :], grad.at[rows, :], b_recv.at[k]).wait()

        total = None
        for r in range(ROWS):
            if nv % 16 == 0:
                g = grad[base + r * nv : base + (r + 1) * nv, 0:NLON]
            else:
                pair = grad[base + (r // 2) * 2 * nv : base + (r // 2 + 1) * 2 * nv, 0:NLON]
                g = pair.astype(F32)[(r % 2) * nv : (r % 2 + 1) * nv].astype(BF16)
            term = jnp.dot(g, featv[r], preferred_element_type=F32)
            total = term if total is None else total + term
        wgp[v0 : v0 + nv, :] = total
        if k > 0:
            for o in range(8) if k == 1 else range(8, OCTETS):
                rows_o = wgp.at[pl.ds(8 * o, 8)]

                @pl.when(me_ey == o)
                def _(rows_o=rows_o):
                    pltpu.make_async_copy(rows_o, wa.at[me_ey], w_recv.at[0]).start()

                @pl.when(me_ey != o)
                def _(rows_o=rows_o, o=o):
                    pltpu.make_async_remote_copy(
                        src_ref=rows_o,
                        dst_ref=wa.at[me_ey],
                        send_sem=w_send.at[o],
                        recv_sem=w_recv.at[0],
                        device_id=ey_device(jnp.int32(o // 2), jnp.int32(o % 2)),
                        device_id_type=MESH,
                    ).start()

        waves = nt_dot(basisv[...], grad[rows, :])
        if k < 2:
            ssend[k][...] = waves.reshape(nlat, MPAD, 128).astype(BF16)
        else:
            s2f[:, 0:32] = waves
            for j in range(6):
                cols = [s2f[pl.ds(6 * g + j, nlat, stride=MPAD), :][:, 0:32] for g in range(4)]
                m2f[pl.ds(j, nlat, stride=8), :] = jnp.concatenate(cols, axis=1)
            ssend[k][...] = m2f[...].reshape(nlat, 8, 128).astype(BF16)

        def send_lat(s, c, k=k):
            dev = lax.rem(me_q + s, nlat)
            pltpu.make_async_remote_copy(
                src_ref=ssend[k].at[dev],
                dst_ref=rout[k].at[me_q],
                send_sem=l_send.at[k],
                recv_sem=l_recv.at[k],
                device_id={"lat": dev},
                device_id_type=MESH,
            ).start()
            return c

        lax.fori_loop(1, nlat, send_lat, 0)
        pltpu.make_async_copy(ssend[k].at[me_q], rout[k].at[me_q], l_recv.at[k]).start()

    def gather(k):
        pltpu.make_async_copy(rout[k], rout[k], l_recv.at[k]).wait()
        if k == 2:
            x2f[...] = rout[k][...].astype(F32).reshape(nlat * 8, 128)
            for j in range(6):
                lhs2[nlat * j : nlat * (j + 1), :] = x2f[pl.ds(j, nlat, stride=8), :]
        else:
            x01[k] = rout[k][...].astype(F32).reshape(nlat * MPAD, 128)
            for i in range(MP):
                lhs01[nlat * i : nlat * (i + 1), 128 * k : 128 * k + 128] = x01[k, pl.ds(i, nlat, stride=MPAD), :].astype(BF16)

    gather(0)

    @pl.when(me_ey < OCTETS)
    def _():
        pltpu.make_async_copy(wa, wa, w_recv.at[0]).wait()
        wsum[0] = jnp.sum(wa[...], axis=0)

        def send_zc(s, c):
            pltpu.make_async_remote_copy(
                src_ref=wsum.at[0],
                dst_ref=wb.at[me_zc],
                send_sem=w_send.at[OCTETS],
                recv_sem=w_recv.at[1],
                device_id=zc_device(lax.rem(me_zc + s, zc_count)),
                device_id_type=MESH,
            ).start()
            return c

        lax.fori_loop(1, zc_count, send_zc, 0)
        pltpu.make_async_copy(wsum.at[0], wb.at[me_zc], w_recv.at[1]).start()

    gather(1)
    gather(2)
    @pl.when(me_ey < OCTETS)
    def _():
        pltpu.make_async_copy(wb, wb, w_recv.at[1]).wait()
        wsum[1] = jnp.sum(wb[...], axis=0)

        def send_ey(s, c):
            i = lax.rem(me_ey + s, ey_count)
            pltpu.make_async_remote_copy(
                src_ref=wsum.at[1],
                dst_ref=wfin.at[me_ey],
                send_sem=w_send.at[OCTETS + 1],
                recv_sem=wc_recv,
                device_id=ey_device(i // 2, lax.rem(i, 2)),
                device_id_type=MESH,
            ).start()
            return c

        lax.fori_loop(1, ey_count, send_ey, 0)
        pltpu.make_async_copy(wsum.at[1], wfin.at[me_ey], wc_recv).start()

    for g in range(4):
        nj = min(6, MP - 6 * g)
        n = nj * nlat
        group = lax.broadcasted_iota(jnp.int32, (n, 128), 1) // 32
        last = jnp.where(group == g, lhs2[0:n, :], 0.0).astype(BF16)
        y = jnp.dot(lhs01[6 * g * nlat : 6 * g * nlat + n, :], bd01[...], preferred_element_type=F32)
        y = y + jnp.dot(last, bd2[...], preferred_element_type=F32)
        for j in range(nj):
            m, p = (6 * g + j) // 2, (6 * g + j) % 2
            for r in range(ROWS):
                at = (p * ROWS + r) * nlat
                ybuf[m, at : at + nlat, :] = y[j * nlat : (j + 1) * nlat, CH * r : CH * r + CH].astype(BF16)

    for m in range(ORDERS_PER):
        res = jnp.dot(t2b[m], ybuf[m], preferred_element_type=F32).astype(BF16)
        spec[0, m] = res.reshape(DEGREES, 2, CH)

    pltpu.make_async_copy(wfin, wfin, wc_recv).wait()
    wg[...] = wfin[...].reshape(NVAR, CH)

    for k in range(3):
        part = frecv[k].at[pl.ds(0, ENS - 1)]
        pltpu.make_async_copy(part, part, f_send.at[k]).wait()
        part = bsend[k].at[pl.ds(0, ENS - 1)]
        pltpu.make_async_copy(part, part, b_send.at[k]).wait()
        part = ssend[k].at[pl.ds(0, nlat - 1)]
        pltpu.make_async_copy(part, part, l_send.at[k]).wait()
    for o in range(OCTETS):

        @pl.when(me_ey != o)
        def _(o=o):
            rows_o = wgp.at[pl.ds(8 * o, 8)]
            pltpu.make_async_copy(rows_o, rows_o, w_send.at[o]).wait()

    @pl.when(me_ey < OCTETS)
    def _():
        part = wb.at[pl.ds(0, zc_count - 1)]
        pltpu.make_async_copy(part, part, w_send.at[OCTETS]).wait()
        part = wa.at[pl.ds(0, ey_count - 1)]
        pltpu.make_async_copy(part, part, w_send.at[OCTETS + 1]).wait()


def local(nlat, features, previous, target, weight, var_weight):
    area, cosine, diag, basis = tables(nlat)
    npts = ROWS * nlat
    nz = nlat // 4
    any_spec = pl.BlockSpec(memory_space=pl.ANY)
    vmem = pl.BlockSpec(memory_space=pltpu.VMEM)
    wt = weight.T
    dma = pltpu.SemaphoreType.DMA
    chunk_rows = [2 * nv for _, nv in VCHUNKS]
    spec, wg = pl.pallas_call(
        functools.partial(first_kernel, nlat),
        out_shape=[
            pltpu.VMEM((1, ORDERS_PER, DEGREES, 2, CH), BF16),
            pltpu.VMEM((NVAR, CH), F32),
        ],
        in_specs=[any_spec] * 3 + [vmem] * 2 + [any_spec] * 2 + [vmem] + [any_spec],
        out_specs=[vmem, vmem],
        scratch_shapes=[
            pltpu.VMEM((ROWS, NLON, CH), BF16),
            pltpu.VMEM((NVAR, ROWS, NLON), BF16),
            pltpu.VMEM((NVAR, ROWS, NLON), BF16),
            pltpu.VMEM((nlat * MPAD, LPAD), BF16),
            pltpu.VMEM((8, 128), F32),
            pltpu.VMEM((16, npts), F32),
            pltpu.VMEM((NTILE, 4 * NVAR, 128), F32),
            pltpu.VMEM((NTILE, 4 * NVAR, 128), F32),
            pltpu.VMEM((4 * NVAR, LPAD), F32),
            pltpu.VMEM((4 * NVAR, LPAD), BF16),
        ]
        + [pltpu.VMEM((ENS, n, LBLK), BF16) for n in chunk_rows] * 2
        + [
            pltpu.VMEM((4 * NVAR, LPAD), BF16),
            pltpu.VMEM((nlat, MPAD, 128), BF16),
            pltpu.VMEM((nlat, MPAD, 128), BF16),
            pltpu.VMEM((nlat, 8, 128), BF16),
            pltpu.VMEM((nlat, MPAD, 128), BF16),
            pltpu.VMEM((nlat, MPAD, 128), BF16),
            pltpu.VMEM((nlat, 8, 128), BF16),
            pltpu.VMEM((nlat * MPAD, 128), F32),
            pltpu.VMEM((nlat * 8, 128), F32),
            pltpu.VMEM((2 * NVAR, LBLK), F32),
            pltpu.VMEM((2 * NVAR, 128), F32),
            pltpu.VMEM((NVAR, CH), F32),
            pltpu.VMEM((2, 8, CH), F32),
            pltpu.VMEM((2 * ENS, 8, CH), F32),
            pltpu.VMEM((2 * nz, 8, CH), F32),
            pltpu.VMEM((OCTETS, 8, CH), F32),
            pltpu.VMEM((DEGREES * 16, npts), F32),
            pltpu.VMEM((2, 2 * DEGREES, npts), F32),
            pltpu.VMEM((ORDERS_PER, 2 * DEGREES, 2 * npts), BF16),
            pltpu.VMEM((2, nlat * MPAD, 128), F32),
            pltpu.VMEM((nlat * 8, 128), F32),
            pltpu.VMEM((256, ROWS * CH), BF16),
            pltpu.VMEM((128, ROWS * CH), F32),
            pltpu.VMEM((128, ROWS * CH), BF16),
            pltpu.VMEM((nlat * MP, 256), BF16),
            pltpu.VMEM((nlat * 6, 128), F32),
            pltpu.VMEM((ORDERS_PER, 2 * npts, CH), BF16),
            dma((9,)), dma((3,)), dma((3,)), dma((3,)), dma((3,)), dma((3,)), dma((3,)),
            dma((OCTETS + 2,)), dma((2,)), dma,
        ],
        compiler_params=pltpu.CompilerParams(
            collective_id=0, has_side_effects=True, vmem_limit_bytes=60 * 1024 * 1024
        ),
        name="loss_and_transform",
    )(features, previous, target, wt, var_weight.reshape(1, NVAR),
      jnp.asarray(basis), jnp.asarray(area), jnp.asarray(cosine), jnp.asarray(diag))

    return spec, wg.T


def solution(mesh):
    placed = (
        P("ens", "lat", None, None),
        P("ens", None, "lat", None),
        P(None, "lat", None),
        P(),
        P(),
    )
    return jax.shard_map(
        functools.partial(local, mesh.shape["lat"]),
        mesh=mesh,
        in_specs=placed,
        out_specs=(P("ens", "lat", None, None, None), P()),
        check_vma=False,
    )
```

```python
import functools
import math

import jax
import jax.numpy as jnp
import ml_dtypes
import numpy as np
from jax import lax
from jax.experimental import pallas as pl
from jax.experimental.pallas import tpu as pltpu
from jax.sharding import PartitionSpec as P

FULL_LAT = 721
DEGREES = 352
ORDERS_PER = 11
MP = 2 * ORDERS_PER
MPAD = 24
ENS = 8
ROWS = 4
NLON = 1440
LPAD = 1536
LBLK = 384
NTILE = LPAD // 128
CH = 256
NVAR = 72
OCTETS = NVAR // 8
VCHUNKS = ((0, 32), (32, 32), (64, 8))

smoothing = 0.1
loss_scale = 2048.0
F32 = jnp.float32
BF16 = jnp.bfloat16
MESH = pl.DeviceIdType.MESH


@functools.lru_cache(maxsize=None)
def tables(lat_count):
    rows = ROWS * lat_count
    first = (FULL_LAT - rows) // 2
    colat = np.pi * (np.arange(rows) + first) / (FULL_LAT - 1)
    total = NLON * np.sum(np.sin(np.pi * np.arange(FULL_LAT) / (FULL_LAT - 1)))
    area = np.zeros((lat_count, 8, 128), np.float32)
    area[:, :ROWS] = (loss_scale * np.sin(colat) / total).reshape(lat_count, ROWS, 1)
    order_of = (np.arange(lat_count)[None, :] * ROWS + np.arange(ROWS)[:, None]).reshape(-1)
    theta = colat[order_of]
    cosine = np.broadcast_to(np.cos(theta), (16, rows)).astype(np.float32)
    count = ORDERS_PER * lat_count
    lg = np.array([math.lgamma(m + 1.5) - math.lgamma(m + 1.0) - math.lgamma(1.5) for m in range(count)])
    diag = np.exp(0.5 * lg[:, None] + np.arange(count)[:, None] * np.log(np.sin(theta))[None, :])
    diag = diag * math.sqrt(0.25 / math.pi)
    diag_table = np.zeros((lat_count, 16, rows), np.float32)
    diag_table[:, :ORDERS_PER] = diag.reshape(lat_count, ORDERS_PER, rows)
    m = np.arange(count)
    j = np.arange(NLON)
    angle = 2.0 * np.pi / NLON * ((m[:, None] * j[None, :]) % NLON)
    ow = np.where(m == 0, 1.0, 2.0)[:, None]
    basis = np.zeros((lat_count, MPAD, LPAD))
    basis[:, 0:MP:2, :NLON] = (ow * np.cos(angle)).reshape(lat_count, ORDERS_PER, NLON)
    basis[:, 1:MP:2, :NLON] = (-ow * np.sin(angle)).reshape(lat_count, ORDERS_PER, NLON)
    basis = basis.reshape(lat_count * MPAD, LPAD).astype(ml_dtypes.bfloat16)
    return area, cosine, diag_table, basis


def softened_slope(delta):
    return delta * lax.rsqrt(delta * delta + smoothing * smoothing)


def nt_dot(a, b):
    return lax.dot_general(a, b, (((1,), (1,)), ((), ())), preferred_element_type=F32)


def first_kernel(
    nlat,
    feat, prev, tgt, wt, vw, basis, area, cosx, diag,
    spec, wg,
    featv, prevv, tgtv, basisv, areav, diagv, prev2, tgt2, fc, fsend,
    fr0, fr1, fr2, bs0, bs1, bs2, grad, ss0, ss1, ss2, rv0, rv1, rv2, s2f, m2f,
    tgo, sco, wgp, wsum, wa, wb, wfin, tleg, t2f, t2b,
    x01, x2f, bd0, bd12, bd2f, lhs0, lhs12, y0, ybuf,
    in_sem, f_send, f_recv, b_send, b_recv, l_send, l_recv, w_send, w_recv, wc_recv,
):
    me_e = lax.axis_index("ens")
    me_q = lax.axis_index("lat")
    npts = ROWS * nlat
    nz = nlat // 4
    me_z, me_y, me_c = me_q // 4, lax.rem(me_q, 4) // 2, lax.rem(me_q, 2)
    zc_count, ey_count = 2 * nz, 2 * ENS
    me_zc, me_ey = me_z * 2 + me_c, me_e * 2 + me_y
    frecv = (fr0, fr1, fr2)
    bsend = (bs0, bs1, bs2)
    ssend = (ss0, ss1, ss2)
    rout = (rv0, rv1, rv2)

    loads = [pltpu.make_async_copy(feat.at[0, r], featv.at[r], in_sem.at[r]) for r in range(ROWS)]
    loads.append(pltpu.make_async_copy(prev.at[0], prevv, in_sem.at[4]))
    loads.append(pltpu.make_async_copy(tgt, tgtv, in_sem.at[5]))
    loads.append(pltpu.make_async_copy(area.at[me_q], areav, in_sem.at[6]))
    loads.append(pltpu.make_async_copy(diag.at[me_q], diagv, in_sem.at[7]))
    loads.append(pltpu.make_async_copy(basis, basisv, in_sem.at[8]))
    for i in (4, 0, 1, 2, 3, 5, 6, 7, 8):
        loads[i].start()

    barrier = pltpu.get_barrier_semaphore()

    def ey_device(ens, y):
        return {"ens": ens, "lat": me_z * 4 + y * 2 + me_c}

    def zc_device(i):
        return {"lat": (i // 2) * 4 + me_y * 2 + lax.rem(i, 2)}

    def greet_ens(s, c):
        pl.semaphore_signal(barrier, inc=1, device_id={"ens": lax.rem(me_e + s, ENS)}, device_id_type=MESH)
        return c

    def greet_lat(s, c):
        pl.semaphore_signal(barrier, inc=1, device_id={"lat": lax.rem(me_q + s, nlat)}, device_id_type=MESH)
        return c

    lax.fori_loop(1, ENS, greet_ens, 0)
    lax.fori_loop(1, nlat, greet_lat, 0)

    def greet_ey(s, c):
        pl.semaphore_signal(
            barrier, inc=1, device_id=ey_device(lax.rem(me_e + s, ENS), 1 - me_y), device_id_type=MESH
        )
        return c

    lax.fori_loop(1, ENS, greet_ey, 0)

    fc[:, LPAD - 128 : LPAD] = jnp.zeros((4 * NVAR, 128), F32)
    prev2[NTILE - 1] = jnp.zeros((4 * NVAR, 128), F32)
    loads[4].wait()

    def widen_prev(i, c):
        pair = jnp.concatenate([prevv[2 * i].astype(F32), prevv[2 * i + 1].astype(F32)], axis=0)
        for lt in range(NTILE):
            wide = min(128, NLON - 128 * lt)
            prev2[lt, pl.ds(pl.multiple_of(8 * i, 8), 8), 0:wide] = pair[:, 128 * lt : 128 * lt + wide]
        return c

    lax.fori_loop(0, NVAR // 2, widen_prev, 0)
    for r in range(ROWS):
        loads[r].wait()
        fc[NVAR * r : NVAR * (r + 1), 0:NLON] = nt_dot(wt[...], featv[r])

    pl.semaphore_wait(barrier, ENS - 1 + nlat - 1 + ENS - 1)

    my_blk = me_e // 2
    my_half = lax.rem(me_e, 2)
    for k, (v0, nv) in enumerate(VCHUNKS):
        base, nh = 4 * v0, 2 * nv
        for lt in range(NTILE):
            lanes = slice(128 * lt, 128 * lt + 128)
            parts = []
            for r in range(ROWS):
                field = fc[NVAR * r + v0 : NVAR * r + v0 + nv, lanes] + prev2[lt, pl.ds(4 * v0 + r, nv, stride=4), :]
                parts.append(field * field * field * jnp.abs(field))
            fsend[base : base + 4 * nv, lanes] = jnp.concatenate(parts, axis=0).astype(BF16)

        def block_of(dev, base=base, nh=nh):
            row = pl.multiple_of(base + lax.rem(dev, 2) * nh, 16)
            lane = pl.multiple_of((dev // 2) * LBLK, 128)
            return pl.ds(row, nh), pl.ds(lane, LBLK)

        def send_fwd(s, c, k=k, block_of=block_of):
            dev = lax.rem(me_e + s, ENS)
            rows, lanes = block_of(dev)
            pltpu.make_async_remote_copy(
                src_ref=fsend.at[rows, lanes],
                dst_ref=frecv[k].at[me_e],
                send_sem=f_send.at[k],
                recv_sem=f_recv.at[k],
                device_id={"ens": dev},
                device_id_type=MESH,
            ).start()
            return c

        lax.fori_loop(1, ENS, send_fwd, 0)
        rows, lanes = block_of(me_e)
        pltpu.make_async_copy(fsend.at[rows, lanes], frecv[k].at[me_e], f_recv.at[k]).start()

    loads[5].wait()
    tgt2[NTILE - 1] = jnp.zeros((4 * NVAR, 128), F32)

    def widen_tgt(i, c):
        pair = jnp.concatenate([tgtv[2 * i].astype(F32), tgtv[2 * i + 1].astype(F32)], axis=0)
        for lt in range(NTILE):
            wide = min(128, NLON - 128 * lt)
            tgt2[lt, pl.ds(pl.multiple_of(8 * i, 8), 8), 0:wide] = pair[:, 128 * lt : 128 * lt + wide]
        return c

    lax.fori_loop(0, NVAR // 2, widen_tgt, 0)
    loads[6].wait()
    lane_id = lax.broadcasted_iota(jnp.int32, (NVAR, NVAR), 1)
    row_id = lax.broadcasted_iota(jnp.int32, (NVAR, NVAR), 0)
    vcol = jnp.sum(jnp.where(lane_id == row_id, vw[...], 0.0), axis=1, keepdims=True)
    my_lane = pl.multiple_of(my_blk * LBLK, 128)
    for k, (v0, nv) in enumerate(VCHUNKS):
        for rr in range(2):
            r = 2 * my_half + rr
            at = 2 * v0 + rr * nv
            for i in range(3):
                tgo[at : at + nv, 128 * i : 128 * i + 128] = tgt2[3 * my_blk + i, pl.ds(4 * v0 + r, nv, stride=4), :]
            sco[at : at + nv, :] = vcol[v0 : v0 + nv] * areav[pl.ds(r, 1), :]

    loads[7].wait()
    order = (lax.broadcasted_iota(jnp.int32, (16, npts), 0) + ORDERS_PER * me_q).astype(F32)
    order_sq = order * order

    def legendre_step(l, carry):
        last, before, eps = carry
        lf = jnp.zeros((16, npts), F32) + l.astype(F32)
        lsq = lf * lf
        gap = lsq - order_sq
        ratio = jnp.maximum(gap, 1.0) / jnp.maximum(4.0 * lsq - 1.0, 1.0)
        inv = lax.rsqrt(ratio)
        new = inv * (cosx[...] * last - eps * before)
        new = jnp.where(lf == order, diagv[...], jnp.where(lf > order, new, 0.0))
        tleg[pl.ds(pl.multiple_of(16 * l, 16), 16), :] = new
        return new, last, jnp.where(gap > 0.0, ratio * inv, 0.0)

    zero = diagv[...] * 0.0
    state = lax.fori_loop(0, DEGREES // 2, legendre_step, (zero, zero, zero), unroll=8)

    for k, (v0, nv) in enumerate(VCHUNKS):
        base, nh = 4 * v0, 2 * nv
        pltpu.make_async_copy(frecv[k], frecv[k], f_recv.at[k]).wait()

        def loss_tile(i, c, k=k, v0=v0):
            row = pl.multiple_of((i // 3) * 16, 16)
            lane = pl.multiple_of(lax.rem(i, 3) * 128, 128)
            fields = []
            for e in range(ENS):
                u = frecv[k][e, pl.ds(row, 16), pl.ds(lane, 128)].astype(F32)
                mag = lax.rsqrt(lax.rsqrt(jnp.abs(u)))
                fields.append(jnp.where(u < 0.0, -mag, mag))
            pair_sum = [None] * ENS
            for a in range(ENS):
                for b in range(a + 1, ENS):
                    s = softened_slope(fields[a] - fields[b])
                    pair_sum[a] = s if pair_sum[a] is None else pair_sum[a] + s
                    pair_sum[b] = -s if pair_sum[b] is None else pair_sum[b] - s
            at = pl.multiple_of(2 * v0 + row, 16)
            aim = tgo[pl.ds(at, 16), pl.ds(lane, 128)]
            scale = sco[pl.ds(at, 16), :]
            for e in range(ENS):
                g = softened_slope(fields[e] - aim) * (1.0 / ENS) - pair_sum[e] * (1.0 / (ENS * (ENS - 1)))
                bsend[k][e, pl.ds(row, 16), pl.ds(lane, 128)] = (scale * g).astype(BF16)
            return c

        lax.fori_loop(0, (nh // 16) * 3, loss_tile, 0)

        my_rows = pl.ds(pl.multiple_of(base + my_half * nh, 16), nh)
        my_lanes = pl.ds(my_lane, LBLK)

        def send_bwd(s, c, k=k, my_rows=my_rows, my_lanes=my_lanes):
            dev = lax.rem(me_e + s, ENS)
            pltpu.make_async_remote_copy(
                src_ref=bsend[k].at[dev],
                dst_ref=grad.at[my_rows, my_lanes],
                send_sem=b_send.at[k],
                recv_sem=b_recv.at[k],
                device_id={"ens": dev},
                device_id_type=MESH,
            ).start()
            return c

        lax.fori_loop(1, ENS, send_bwd, 0)
        pltpu.make_async_copy(bsend[k].at[me_e], grad.at[my_rows, my_lanes], b_recv.at[k]).start()
        if k == 0:
            lax.fori_loop(DEGREES // 2, DEGREES, legendre_step, state, unroll=8)

    t2f[...] = jnp.zeros(t2f.shape, F32)

    def spread(m, c):
        rows = tleg[pl.ds(m, DEGREES, stride=16), :]
        for p in range(2):
            t2f[p, pl.ds(p, DEGREES, stride=2), :] = rows
            t2b[m, :, npts * p : npts * (p + 1)] = t2f[p].astype(BF16)
        return c

    lax.fori_loop(0, ORDERS_PER, spread, 0)

    bd0[...] = jnp.zeros(bd0.shape, BF16)
    bd12[...] = jnp.zeros(bd12.shape, BF16)
    bd2f[...] = jnp.zeros(bd2f.shape, F32)
    tail = wt[64:72, :].astype(F32)
    for r in range(ROWS):
        bd0[32 * r : 32 * r + 32, CH * r : CH * r + CH] = wt[0:32, :]
        bd12[32 * r : 32 * r + 32, CH * r : CH * r + CH] = wt[32:64, :]
        for g in range(4):
            bd2f[32 * g + 8 * r : 32 * g + 8 * r + 8, CH * r : CH * r + CH] = tail
    bd12[128:256, :] = bd2f[...].astype(BF16)

    loads[8].wait()
    m2f[...] = jnp.zeros(m2f.shape, F32)
    for k, (v0, nv) in enumerate(VCHUNKS):
        base = 4 * v0
        rows = pl.ds(base, 4 * nv)
        pltpu.make_async_copy(grad.at[rows, :], grad.at[rows, :], b_recv.at[k]).wait()

        total = None
        for r in range(ROWS):
            if nv % 16 == 0:
                g = grad[base + r * nv : base + (r + 1) * nv, 0:NLON]
            else:
                pair = grad[base + (r // 2) * 2 * nv : base + (r // 2 + 1) * 2 * nv, 0:NLON]
                g = pair.astype(F32)[(r % 2) * nv : (r % 2 + 1) * nv].astype(BF16)
            term = jnp.dot(g, featv[r], preferred_element_type=F32)
            total = term if total is None else total + term
        wgp[v0 : v0 + nv, :] = total
        if k > 0:
            for o in range(8) if k == 1 else range(8, OCTETS):
                rows_o = wgp.at[pl.ds(8 * o, 8)]

                @pl.when(me_ey == o)
                def _(rows_o=rows_o):
                    pltpu.make_async_copy(rows_o, wa.at[me_ey], w_recv.at[0]).start()

                @pl.when(me_ey != o)
                def _(rows_o=rows_o, o=o):
                    pltpu.make_async_remote_copy(
                        src_ref=rows_o,
                        dst_ref=wa.at[me_ey],
                        send_sem=w_send.at[o],
                        recv_sem=w_recv.at[0],
                        device_id=ey_device(jnp.int32(o // 2), jnp.int32(o % 2)),
                        device_id_type=MESH,
                    ).start()

        waves = nt_dot(basisv[...], grad[rows, :])
        if k < 2:
            ssend[k][...] = waves.reshape(nlat, MPAD, 128).astype(BF16)
        else:
            s2f[:, 0:32] = waves
            for j in range(6):
                cols = [s2f[pl.ds(6 * g + j, nlat, stride=MPAD), :][:, 0:32] for g in range(4)]
                m2f[pl.ds(j, nlat, stride=8), :] = jnp.concatenate(cols, axis=1)
            ssend[k][...] = m2f[...].reshape(nlat, 8, 128).astype(BF16)

        def send_lat(s, c, k=k):
            dev = lax.rem(me_q + s, nlat)
            pltpu.make_async_remote_copy(
                src_ref=ssend[k].at[dev],
                dst_ref=rout[k].at[me_q],
                send_sem=l_send.at[k],
                recv_sem=l_recv.at[k],
                device_id={"lat": dev},
                device_id_type=MESH,
            ).start()
            return c

        lax.fori_loop(1, nlat, send_lat, 0)
        pltpu.make_async_copy(ssend[k].at[me_q], rout[k].at[me_q], l_recv.at[k]).start()

    def gather(k):
        pltpu.make_async_copy(rout[k], rout[k], l_recv.at[k]).wait()
        if k == 2:
            x2f[...] = rout[k][...].astype(F32).reshape(nlat * 8, 128)
            group = lax.broadcasted_iota(jnp.int32, (nlat, 128), 1) // 32
            for i in range(MP):
                rows_i = jnp.where(group == i // 6, x2f[pl.ds(i % 6, nlat, stride=8), :], 0.0)
                lhs12[nlat * i : nlat * (i + 1), 128:256] = rows_i.astype(BF16)
        else:
            x01[k] = rout[k][...].astype(F32).reshape(nlat * MPAD, 128)
            for i in range(MP):
                rows_i = x01[k, pl.ds(i, nlat, stride=MPAD), :].astype(BF16)
                if k == 0:
                    lhs0[nlat * i : nlat * (i + 1), :] = rows_i
                else:
                    lhs12[nlat * i : nlat * (i + 1), 0:128] = rows_i

    gather(0)
    y0[...] = jnp.dot(lhs0[...], bd0[...], preferred_element_type=F32)

    @pl.when(me_ey < OCTETS)
    def _():
        pltpu.make_async_copy(wa, wa, w_recv.at[0]).wait()
        wsum[0] = jnp.sum(wa[...], axis=0)

        def send_zc(s, c):
            pltpu.make_async_remote_copy(
                src_ref=wsum.at[0],
                dst_ref=wb.at[me_zc],
                send_sem=w_send.at[OCTETS],
                recv_sem=w_recv.at[1],
                device_id=zc_device(lax.rem(me_zc + s, zc_count)),
                device_id_type=MESH,
            ).start()
            return c

        lax.fori_loop(1, zc_count, send_zc, 0)
        pltpu.make_async_copy(wsum.at[0], wb.at[me_zc], w_recv.at[1]).start()

    gather(1)
    gather(2)
    @pl.when(me_ey < OCTETS)
    def _():
        pltpu.make_async_copy(wb, wb, w_recv.at[1]).wait()
        wsum[1] = jnp.sum(wb[...], axis=0)

        def send_ey(s, c):
            i = lax.rem(me_ey + s, ey_count)
            pltpu.make_async_remote_copy(
                src_ref=wsum.at[1],
                dst_ref=wfin.at[me_ey],
                send_sem=w_send.at[OCTETS + 1],
                recv_sem=wc_recv,
                device_id=ey_device(i // 2, lax.rem(i, 2)),
                device_id_type=MESH,
            ).start()
            return c

        lax.fori_loop(1, ey_count, send_ey, 0)
        pltpu.make_async_copy(wsum.at[1], wfin.at[me_ey], wc_recv).start()

    for i in range(0, MP, 2):
        rows_m = slice(nlat * i, nlat * (i + 2))
        y = y0[rows_m, :] + jnp.dot(lhs12[rows_m, :], bd12[...], preferred_element_type=F32)
        for p in range(2):
            for r in range(ROWS):
                at = (p * ROWS + r) * nlat
                block = y[p * nlat : (p + 1) * nlat, CH * r : CH * r + CH]
                ybuf[i // 2, at : at + nlat, :] = block.astype(BF16)

    for m in range(ORDERS_PER):
        res = jnp.dot(t2b[m], ybuf[m], preferred_element_type=F32).astype(BF16)
        spec[0, m] = res.reshape(DEGREES, 2, CH)

    pltpu.make_async_copy(wfin, wfin, wc_recv).wait()
    wg[...] = wfin[...].reshape(NVAR, CH)

    for k in range(3):
        part = frecv[k].at[pl.ds(0, ENS - 1)]
        pltpu.make_async_copy(part, part, f_send.at[k]).wait()
        part = bsend[k].at[pl.ds(0, ENS - 1)]
        pltpu.make_async_copy(part, part, b_send.at[k]).wait()
        part = ssend[k].at[pl.ds(0, nlat - 1)]
        pltpu.make_async_copy(part, part, l_send.at[k]).wait()
    for o in range(OCTETS):

        @pl.when(me_ey != o)
        def _(o=o):
            rows_o = wgp.at[pl.ds(8 * o, 8)]
            pltpu.make_async_copy(rows_o, rows_o, w_send.at[o]).wait()

    @pl.when(me_ey < OCTETS)
    def _():
        part = wb.at[pl.ds(0, zc_count - 1)]
        pltpu.make_async_copy(part, part, w_send.at[OCTETS]).wait()
        part = wa.at[pl.ds(0, ey_count - 1)]
        pltpu.make_async_copy(part, part, w_send.at[OCTETS + 1]).wait()


def local(nlat, features, previous, target, weight, var_weight):
    area, cosine, diag, basis = tables(nlat)
    npts = ROWS * nlat
    nz = nlat // 4
    any_spec = pl.BlockSpec(memory_space=pl.ANY)
    vmem = pl.BlockSpec(memory_space=pltpu.VMEM)
    wt = weight.T
    dma = pltpu.SemaphoreType.DMA
    chunk_rows = [2 * nv for _, nv in VCHUNKS]
    spec, wg = pl.pallas_call(
        functools.partial(first_kernel, nlat),
        out_shape=[
            pltpu.VMEM((1, ORDERS_PER, DEGREES, 2, CH), BF16),
            pltpu.VMEM((NVAR, CH), F32),
        ],
        in_specs=[any_spec] * 3 + [vmem] * 2 + [any_spec] * 2 + [vmem] + [any_spec],
        out_specs=[vmem, vmem],
        scratch_shapes=[
            pltpu.VMEM((ROWS, NLON, CH), BF16),
            pltpu.VMEM((NVAR, ROWS, NLON), BF16),
            pltpu.VMEM((NVAR, ROWS, NLON), BF16),
            pltpu.VMEM((nlat * MPAD, LPAD), BF16),
            pltpu.VMEM((8, 128), F32),
            pltpu.VMEM((16, npts), F32),
            pltpu.VMEM((NTILE, 4 * NVAR, 128), F32),
            pltpu.VMEM((NTILE, 4 * NVAR, 128), F32),
            pltpu.VMEM((4 * NVAR, LPAD), F32),
            pltpu.VMEM((4 * NVAR, LPAD), BF16),
        ]
        + [pltpu.VMEM((ENS, n, LBLK), BF16) for n in chunk_rows] * 2
        + [
            pltpu.VMEM((4 * NVAR, LPAD), BF16),
            pltpu.VMEM((nlat, MPAD, 128), BF16),
            pltpu.VMEM((nlat, MPAD, 128), BF16),
            pltpu.VMEM((nlat, 8, 128), BF16),
            pltpu.VMEM((nlat, MPAD, 128), BF16),
            pltpu.VMEM((nlat, MPAD, 128), BF16),
            pltpu.VMEM((nlat, 8, 128), BF16),
            pltpu.VMEM((nlat * MPAD, 128), F32),
            pltpu.VMEM((nlat * 8, 128), F32),
            pltpu.VMEM((2 * NVAR, LBLK), F32),
            pltpu.VMEM((2 * NVAR, 128), F32),
            pltpu.VMEM((NVAR, CH), F32),
            pltpu.VMEM((2, 8, CH), F32),
            pltpu.VMEM((2 * ENS, 8, CH), F32),
            pltpu.VMEM((2 * nz, 8, CH), F32),
            pltpu.VMEM((OCTETS, 8, CH), F32),
            pltpu.VMEM((DEGREES * 16, npts), F32),
            pltpu.VMEM((2, 2 * DEGREES, npts), F32),
            pltpu.VMEM((ORDERS_PER, 2 * DEGREES, 2 * npts), BF16),
            pltpu.VMEM((2, nlat * MPAD, 128), F32),
            pltpu.VMEM((nlat * 8, 128), F32),
            pltpu.VMEM((128, ROWS * CH), BF16),
            pltpu.VMEM((256, ROWS * CH), BF16),
            pltpu.VMEM((128, ROWS * CH), F32),
            pltpu.VMEM((nlat * MP, 128), BF16),
            pltpu.VMEM((nlat * MP, 256), BF16),
            pltpu.VMEM((nlat * MP, ROWS * CH), F32),
            pltpu.VMEM((ORDERS_PER, 2 * npts, CH), BF16),
            dma((9,)), dma((3,)), dma((3,)), dma((3,)), dma((3,)), dma((3,)), dma((3,)),
            dma((OCTETS + 2,)), dma((2,)), dma,
        ],
        compiler_params=pltpu.CompilerParams(
            collective_id=0, has_side_effects=True, vmem_limit_bytes=60 * 1024 * 1024
        ),
        name="loss_and_transform",
    )(features, previous, target, wt, var_weight.reshape(1, NVAR),
      jnp.asarray(basis), jnp.asarray(area), jnp.asarray(cosine), jnp.asarray(diag))

    return spec, wg.T


def solution(mesh):
    placed = (
        P("ens", "lat", None, None),
        P("ens", None, "lat", None),
        P(None, "lat", None),
        P(),
        P(),
    )
    return jax.shard_map(
        functools.partial(local, mesh.shape["lat"]),
        mesh=mesh,
        in_specs=placed,
        out_specs=(P("ens", "lat", None, None, None), P()),
        check_vma=False,
    )
```

```python
import functools
import math

import jax
import jax.numpy as jnp
import ml_dtypes
import numpy as np
from jax import lax
from jax.experimental import pallas as pl
from jax.experimental.pallas import tpu as pltpu
from jax.sharding import PartitionSpec as P

FULL_LAT = 721
DEGREES = 352
ORDERS_PER = 11
MP = 2 * ORDERS_PER
MPAD = 24
ENS = 8
ROWS = 4
NLON = 1440
LPAD = 1536
LBLK = 384
NTILE = LPAD // 128
CH = 256
NVAR = 72
OCTETS = NVAR // 8
VCHUNKS = ((0, 32), (32, 32), (64, 8))

smoothing = 0.1
loss_scale = 2048.0
F32 = jnp.float32
BF16 = jnp.bfloat16
MESH = pl.DeviceIdType.MESH


@functools.lru_cache(maxsize=None)
def tables(lat_count):
    rows = ROWS * lat_count
    first = (FULL_LAT - rows) // 2
    colat = np.pi * (np.arange(rows) + first) / (FULL_LAT - 1)
    total = NLON * np.sum(np.sin(np.pi * np.arange(FULL_LAT) / (FULL_LAT - 1)))
    area = np.zeros((lat_count, 8, 128), np.float32)
    area[:, :ROWS] = (loss_scale * np.sin(colat) / total).reshape(lat_count, ROWS, 1)
    order_of = (np.arange(lat_count)[None, :] * ROWS + np.arange(ROWS)[:, None]).reshape(-1)
    theta = colat[order_of]
    cosine = np.broadcast_to(np.cos(theta), (16, rows)).astype(np.float32)
    count = ORDERS_PER * lat_count
    lg = np.array([math.lgamma(m + 1.5) - math.lgamma(m + 1.0) - math.lgamma(1.5) for m in range(count)])
    diag = np.exp(0.5 * lg[:, None] + np.arange(count)[:, None] * np.log(np.sin(theta))[None, :])
    diag = diag * math.sqrt(0.25 / math.pi)
    diag_table = np.zeros((lat_count, 16, rows), np.float32)
    diag_table[:, :ORDERS_PER] = diag.reshape(lat_count, ORDERS_PER, rows)
    m = np.arange(count)
    j = np.arange(NLON)
    angle = 2.0 * np.pi / NLON * ((m[:, None] * j[None, :]) % NLON)
    ow = np.where(m == 0, 1.0, 2.0)[:, None]
    basis = np.zeros((lat_count, MPAD, LPAD))
    basis[:, 0:MP:2, :NLON] = (ow * np.cos(angle)).reshape(lat_count, ORDERS_PER, NLON)
    basis[:, 1:MP:2, :NLON] = (-ow * np.sin(angle)).reshape(lat_count, ORDERS_PER, NLON)
    basis = basis.reshape(lat_count * MPAD, LPAD).astype(ml_dtypes.bfloat16)
    return area, cosine, diag_table, basis


def softened_slope(delta):
    return delta * lax.rsqrt(delta * delta + smoothing * smoothing)


def nt_dot(a, b):
    return lax.dot_general(a, b, (((1,), (1,)), ((), ())), preferred_element_type=F32)


def first_kernel(
    nlat,
    feat, prev, tgt, wt, vw, basis, area, cosx, diag,
    spec, wg,
    featv, prevv, tgtv, basisv, areav, diagv, prev2, tgt2, fc, fsend,
    fr0, fr1, fr2, bs0, bs1, bs2, grad, ss0, ss1, ss2, rv0, rv1, rv2, s2f, m2f,
    tgo, sco, wgp, wsum, wa, wb, wfin, tleg, t2f, t2b,
    x01, x2f, bd0, bd12, bd2f, lhs0, lhs12, y0, ybuf,
    in_sem, f_send, f_recv, b_send, b_recv, l_send, l_recv, w_send, w_recv, wc_recv,
):
    me_e = lax.axis_index("ens")
    me_q = lax.axis_index("lat")
    npts = ROWS * nlat
    nz = nlat // 4
    me_z, me_y, me_c = me_q // 4, lax.rem(me_q, 4) // 2, lax.rem(me_q, 2)
    zc_count, ey_count = 2 * nz, 2 * ENS
    me_zc, me_ey = me_z * 2 + me_c, me_e * 2 + me_y
    frecv = (fr0, fr1, fr2)
    bsend = (bs0, bs1, bs2)
    ssend = (ss0, ss1, ss2)
    rout = (rv0, rv1, rv2)

    loads = [pltpu.make_async_copy(feat.at[0, r], featv.at[r], in_sem.at[r]) for r in range(ROWS)]
    loads.append(pltpu.make_async_copy(prev.at[0], prevv, in_sem.at[4]))
    loads.append(pltpu.make_async_copy(tgt, tgtv, in_sem.at[5]))
    loads.append(pltpu.make_async_copy(area.at[me_q], areav, in_sem.at[6]))
    loads.append(pltpu.make_async_copy(diag.at[me_q], diagv, in_sem.at[7]))
    loads.append(pltpu.make_async_copy(basis, basisv, in_sem.at[8]))
    for i in (4, 0, 1, 2, 3, 5, 6, 7, 8):
        loads[i].start()

    barrier = pltpu.get_barrier_semaphore()

    def ey_device(ens, y):
        return {"ens": ens, "lat": me_z * 4 + y * 2 + me_c}

    def zc_device(i):
        return {"lat": (i // 2) * 4 + me_y * 2 + lax.rem(i, 2)}

    def greet_ens(s, c):
        pl.semaphore_signal(barrier, inc=1, device_id={"ens": lax.rem(me_e + s, ENS)}, device_id_type=MESH)
        return c

    def greet_lat(s, c):
        pl.semaphore_signal(barrier, inc=1, device_id={"lat": lax.rem(me_q + s, nlat)}, device_id_type=MESH)
        return c

    lax.fori_loop(1, ENS, greet_ens, 0)
    lax.fori_loop(1, nlat, greet_lat, 0)

    def greet_ey(s, c):
        pl.semaphore_signal(
            barrier, inc=1, device_id=ey_device(lax.rem(me_e + s, ENS), 1 - me_y), device_id_type=MESH
        )
        return c

    lax.fori_loop(1, ENS, greet_ey, 0)

    fc[:, LPAD - 128 : LPAD] = jnp.zeros((4 * NVAR, 128), F32)
    prev2[NTILE - 1] = jnp.zeros((4 * NVAR, 128), F32)
    loads[4].wait()

    def widen_prev(i, c):
        pair = jnp.concatenate([prevv[2 * i].astype(F32), prevv[2 * i + 1].astype(F32)], axis=0)
        for lt in range(NTILE):
            wide = min(128, NLON - 128 * lt)
            prev2[lt, pl.ds(pl.multiple_of(8 * i, 8), 8), 0:wide] = pair[:, 128 * lt : 128 * lt + wide]
        return c

    lax.fori_loop(0, NVAR // 2, widen_prev, 0)
    for r in range(ROWS):
        loads[r].wait()
        fc[NVAR * r : NVAR * (r + 1), 0:NLON] = nt_dot(wt[...], featv[r])

    pl.semaphore_wait(barrier, ENS - 1 + nlat - 1 + ENS - 1)

    my_blk = me_e // 2
    my_half = lax.rem(me_e, 2)
    for k, (v0, nv) in enumerate(VCHUNKS):
        base, nh = 4 * v0, 2 * nv
        for lt in range(NTILE):
            lanes = slice(128 * lt, 128 * lt + 128)
            parts = []
            for r in range(ROWS):
                field = fc[NVAR * r + v0 : NVAR * r + v0 + nv, lanes] + prev2[lt, pl.ds(4 * v0 + r, nv, stride=4), :]
                square = field * field
                parts.append((square * square) * (square * (field * jnp.abs(field))))
            fsend[base : base + 4 * nv, lanes] = jnp.concatenate(parts, axis=0).astype(BF16)

        def block_of(dev, base=base, nh=nh):
            row = pl.multiple_of(base + lax.rem(dev, 2) * nh, 16)
            lane = pl.multiple_of((dev // 2) * LBLK, 128)
            return pl.ds(row, nh), pl.ds(lane, LBLK)

        def send_fwd(s, c, k=k, block_of=block_of):
            dev = lax.rem(me_e + s, ENS)
            rows, lanes = block_of(dev)
            pltpu.make_async_remote_copy(
                src_ref=fsend.at[rows, lanes],
                dst_ref=frecv[k].at[me_e],
                send_sem=f_send.at[k],
                recv_sem=f_recv.at[k],
                device_id={"ens": dev},
                device_id_type=MESH,
            ).start()
            return c

        lax.fori_loop(1, ENS, send_fwd, 0)
        rows, lanes = block_of(me_e)
        pltpu.make_async_copy(fsend.at[rows, lanes], frecv[k].at[me_e], f_recv.at[k]).start()

    loads[5].wait()
    tgt2[NTILE - 1] = jnp.zeros((4 * NVAR, 128), F32)

    def widen_tgt(i, c):
        pair = jnp.concatenate([tgtv[2 * i].astype(F32), tgtv[2 * i + 1].astype(F32)], axis=0)
        for lt in range(NTILE):
            wide = min(128, NLON - 128 * lt)
            tgt2[lt, pl.ds(pl.multiple_of(8 * i, 8), 8), 0:wide] = pair[:, 128 * lt : 128 * lt + wide]
        return c

    lax.fori_loop(0, NVAR // 2, widen_tgt, 0)
    loads[6].wait()
    lane_id = lax.broadcasted_iota(jnp.int32, (NVAR, NVAR), 1)
    row_id = lax.broadcasted_iota(jnp.int32, (NVAR, NVAR), 0)
    vcol = jnp.sum(jnp.where(lane_id == row_id, vw[...], 0.0), axis=1, keepdims=True)
    my_lane = pl.multiple_of(my_blk * LBLK, 128)
    for k, (v0, nv) in enumerate(VCHUNKS):
        for rr in range(2):
            r = 2 * my_half + rr
            at = 2 * v0 + rr * nv
            for i in range(3):
                tgo[at : at + nv, 128 * i : 128 * i + 128] = tgt2[3 * my_blk + i, pl.ds(4 * v0 + r, nv, stride=4), :]
            sco[at : at + nv, :] = vcol[v0 : v0 + nv] * areav[pl.ds(r, 1), :]

    loads[7].wait()
    order = (lax.broadcasted_iota(jnp.int32, (16, npts), 0) + ORDERS_PER * me_q).astype(F32)
    order_sq = order * order

    def legendre_step(l, carry):
        last, before, eps = carry
        lf = jnp.zeros((16, npts), F32) + l.astype(F32)
        lsq = lf * lf
        gap = lsq - order_sq
        ratio = jnp.maximum(gap, 1.0) / jnp.maximum(4.0 * lsq - 1.0, 1.0)
        inv = lax.rsqrt(ratio)
        new = inv * (cosx[...] * last - eps * before)
        new = jnp.where(lf == order, diagv[...], jnp.where(lf > order, new, 0.0))
        tleg[pl.ds(pl.multiple_of(16 * l, 16), 16), :] = new
        return new, last, jnp.where(gap > 0.0, ratio * inv, 0.0)

    zero = diagv[...] * 0.0
    state = lax.fori_loop(0, DEGREES // 2, legendre_step, (zero, zero, zero), unroll=8)

    for k, (v0, nv) in enumerate(VCHUNKS):
        base, nh = 4 * v0, 2 * nv
        pltpu.make_async_copy(frecv[k], frecv[k], f_recv.at[k]).wait()

        def loss_tile(i, c, k=k, v0=v0):
            row = pl.multiple_of((i // 3) * 16, 16)
            lane = pl.multiple_of(lax.rem(i, 3) * 128, 128)
            fields = []
            for e in range(ENS):
                u = frecv[k][e, pl.ds(row, 16), pl.ds(lane, 128)].astype(F32)
                root = lax.rsqrt(lax.rsqrt(jnp.abs(u)))
                mag = root * lax.rsqrt(jnp.maximum(root, 1e-30))
                fields.append(jnp.where(u < 0.0, -mag, mag))
            pair_sum = [None] * ENS
            for a in range(ENS):
                for b in range(a + 1, ENS):
                    s = softened_slope(fields[a] - fields[b])
                    pair_sum[a] = s if pair_sum[a] is None else pair_sum[a] + s
                    pair_sum[b] = -s if pair_sum[b] is None else pair_sum[b] - s
            at = pl.multiple_of(2 * v0 + row, 16)
            aim = tgo[pl.ds(at, 16), pl.ds(lane, 128)]
            scale = sco[pl.ds(at, 16), :]
            for e in range(ENS):
                g = softened_slope(fields[e] - aim) * (1.0 / ENS) - pair_sum[e] * (1.0 / (ENS * (ENS - 1)))
                bsend[k][e, pl.ds(row, 16), pl.ds(lane, 128)] = (scale * g).astype(BF16)
            return c

        lax.fori_loop(0, (nh // 16) * 3, loss_tile, 0)

        my_rows = pl.ds(pl.multiple_of(base + my_half * nh, 16), nh)
        my_lanes = pl.ds(my_lane, LBLK)

        def send_bwd(s, c, k=k, my_rows=my_rows, my_lanes=my_lanes):
            dev = lax.rem(me_e + s, ENS)
            pltpu.make_async_remote_copy(
                src_ref=bsend[k].at[dev],
                dst_ref=grad.at[my_rows, my_lanes],
                send_sem=b_send.at[k],
                recv_sem=b_recv.at[k],
                device_id={"ens": dev},
                device_id_type=MESH,
            ).start()
            return c

        lax.fori_loop(1, ENS, send_bwd, 0)
        pltpu.make_async_copy(bsend[k].at[me_e], grad.at[my_rows, my_lanes], b_recv.at[k]).start()
        if k == 0:
            lax.fori_loop(DEGREES // 2, DEGREES, legendre_step, state, unroll=8)

    t2f[...] = jnp.zeros(t2f.shape, F32)

    def spread(m, c):
        rows = tleg[pl.ds(m, DEGREES, stride=16), :]
        for p in range(2):
            t2f[p, pl.ds(p, DEGREES, stride=2), :] = rows
            t2b[m, :, npts * p : npts * (p + 1)] = t2f[p].astype(BF16)
        return c

    lax.fori_loop(0, ORDERS_PER, spread, 0)

    bd0[...] = jnp.zeros(bd0.shape, BF16)
    bd12[...] = jnp.zeros(bd12.shape, BF16)
    bd2f[...] = jnp.zeros(bd2f.shape, F32)
    tail = wt[64:72, :].astype(F32)
    for r in range(ROWS):
        bd0[32 * r : 32 * r + 32, CH * r : CH * r + CH] = wt[0:32, :]
        bd12[32 * r : 32 * r + 32, CH * r : CH * r + CH] = wt[32:64, :]
        for g in range(4):
            bd2f[32 * g + 8 * r : 32 * g + 8 * r + 8, CH * r : CH * r + CH] = tail
    bd12[128:256, :] = bd2f[...].astype(BF16)

    loads[8].wait()
    m2f[...] = jnp.zeros(m2f.shape, F32)
    for k, (v0, nv) in enumerate(VCHUNKS):
        base = 4 * v0
        rows = pl.ds(base, 4 * nv)
        pltpu.make_async_copy(grad.at[rows, :], grad.at[rows, :], b_recv.at[k]).wait()

        total = None
        for r in range(ROWS):
            if nv % 16 == 0:
                g = grad[base + r * nv : base + (r + 1) * nv, 0:NLON]
            else:
                pair = grad[base + (r // 2) * 2 * nv : base + (r // 2 + 1) * 2 * nv, 0:NLON]
                g = pair.astype(F32)[(r % 2) * nv : (r % 2 + 1) * nv].astype(BF16)
            term = jnp.dot(g, featv[r], preferred_element_type=F32)
            total = term if total is None else total + term
        wgp[v0 : v0 + nv, :] = total
        if k > 0:
            for o in range(8) if k == 1 else range(8, OCTETS):
                rows_o = wgp.at[pl.ds(8 * o, 8)]

                @pl.when(me_ey == o)
                def _(rows_o=rows_o):
                    pltpu.make_async_copy(rows_o, wa.at[me_ey], w_recv.at[0]).start()

                @pl.when(me_ey != o)
                def _(rows_o=rows_o, o=o):
                    pltpu.make_async_remote_copy(
                        src_ref=rows_o,
                        dst_ref=wa.at[me_ey],
                        send_sem=w_send.at[o],
                        recv_sem=w_recv.at[0],
                        device_id=ey_device(jnp.int32(o // 2), jnp.int32(o % 2)),
                        device_id_type=MESH,
                    ).start()

        waves = nt_dot(basisv[...], grad[rows, :])
        if k < 2:
            ssend[k][...] = waves.reshape(nlat, MPAD, 128).astype(BF16)
        else:
            s2f[:, 0:32] = waves
            for j in range(6):
                cols = [s2f[pl.ds(6 * g + j, nlat, stride=MPAD), :][:, 0:32] for g in range(4)]
                m2f[pl.ds(j, nlat, stride=8), :] = jnp.concatenate(cols, axis=1)
            ssend[k][...] = m2f[...].reshape(nlat, 8, 128).astype(BF16)

        def send_lat(s, c, k=k):
            dev = lax.rem(me_q + s, nlat)
            pltpu.make_async_remote_copy(
                src_ref=ssend[k].at[dev],
                dst_ref=rout[k].at[me_q],
                send_sem=l_send.at[k],
                recv_sem=l_recv.at[k],
                device_id={"lat": dev},
                device_id_type=MESH,
            ).start()
            return c

        lax.fori_loop(1, nlat, send_lat, 0)
        pltpu.make_async_copy(ssend[k].at[me_q], rout[k].at[me_q], l_recv.at[k]).start()

    def gather(k):
        pltpu.make_async_copy(rout[k], rout[k], l_recv.at[k]).wait()
        if k == 2:
            x2f[...] = rout[k][...].astype(F32).reshape(nlat * 8, 128)
            group = lax.broadcasted_iota(jnp.int32, (nlat, 128), 1) // 32
            for i in range(MP):
                rows_i = jnp.where(group == i // 6, x2f[pl.ds(i % 6, nlat, stride=8), :], 0.0)
                lhs12[nlat * i : nlat * (i + 1), 128:256] = rows_i.astype(BF16)
        else:
            x01[k] = rout[k][...].astype(F32).reshape(nlat * MPAD, 128)
            for i in range(MP):
                rows_i = x01[k, pl.ds(i, nlat, stride=MPAD), :].astype(BF16)
                if k == 0:
                    lhs0[nlat * i : nlat * (i + 1), :] = rows_i
                else:
                    lhs12[nlat * i : nlat * (i + 1), 0:128] = rows_i

    gather(0)
    y0[...] = jnp.dot(lhs0[...], bd0[...], preferred_element_type=F32)

    @pl.when(me_ey < OCTETS)
    def _():
        pltpu.make_async_copy(wa, wa, w_recv.at[0]).wait()
        wsum[0] = jnp.sum(wa[...], axis=0)

        def send_zc(s, c):
            pltpu.make_async_remote_copy(
                src_ref=wsum.at[0],
                dst_ref=wb.at[me_zc],
                send_sem=w_send.at[OCTETS],
                recv_sem=w_recv.at[1],
                device_id=zc_device(lax.rem(me_zc + s, zc_count)),
                device_id_type=MESH,
            ).start()
            return c

        lax.fori_loop(1, zc_count, send_zc, 0)
        pltpu.make_async_copy(wsum.at[0], wb.at[me_zc], w_recv.at[1]).start()

    gather(1)
    gather(2)
    @pl.when(me_ey < OCTETS)
    def _():
        pltpu.make_async_copy(wb, wb, w_recv.at[1]).wait()
        wsum[1] = jnp.sum(wb[...], axis=0)

        def send_ey(s, c):
            i = lax.rem(me_ey + s, ey_count)
            pltpu.make_async_remote_copy(
                src_ref=wsum.at[1],
                dst_ref=wfin.at[me_ey],
                send_sem=w_send.at[OCTETS + 1],
                recv_sem=wc_recv,
                device_id=ey_device(i // 2, lax.rem(i, 2)),
                device_id_type=MESH,
            ).start()
            return c

        lax.fori_loop(1, ey_count, send_ey, 0)
        pltpu.make_async_copy(wsum.at[1], wfin.at[me_ey], wc_recv).start()

    for i in range(0, MP, 2):
        rows_m = slice(nlat * i, nlat * (i + 2))
        y = y0[rows_m, :] + jnp.dot(lhs12[rows_m, :], bd12[...], preferred_element_type=F32)
        for p in range(2):
            for r in range(ROWS):
                at = (p * ROWS + r) * nlat
                block = y[p * nlat : (p + 1) * nlat, CH * r : CH * r + CH]
                ybuf[i // 2, at : at + nlat, :] = block.astype(BF16)

    for m in range(ORDERS_PER):
        res = jnp.dot(t2b[m], ybuf[m], preferred_element_type=F32).astype(BF16)
        spec[0, m] = res.reshape(DEGREES, 2, CH)

    pltpu.make_async_copy(wfin, wfin, wc_recv).wait()
    wg[...] = wfin[...].reshape(NVAR, CH)

    for k in range(3):
        part = frecv[k].at[pl.ds(0, ENS - 1)]
        pltpu.make_async_copy(part, part, f_send.at[k]).wait()
        part = bsend[k].at[pl.ds(0, ENS - 1)]
        pltpu.make_async_copy(part, part, b_send.at[k]).wait()
        part = ssend[k].at[pl.ds(0, nlat - 1)]
        pltpu.make_async_copy(part, part, l_send.at[k]).wait()
    for o in range(OCTETS):

        @pl.when(me_ey != o)
        def _(o=o):
            rows_o = wgp.at[pl.ds(8 * o, 8)]
            pltpu.make_async_copy(rows_o, rows_o, w_send.at[o]).wait()

    @pl.when(me_ey < OCTETS)
    def _():
        part = wb.at[pl.ds(0, zc_count - 1)]
        pltpu.make_async_copy(part, part, w_send.at[OCTETS]).wait()
        part = wa.at[pl.ds(0, ey_count - 1)]
        pltpu.make_async_copy(part, part, w_send.at[OCTETS + 1]).wait()


def local(nlat, features, previous, target, weight, var_weight):
    area, cosine, diag, basis = tables(nlat)
    npts = ROWS * nlat
    nz = nlat // 4
    any_spec = pl.BlockSpec(memory_space=pl.ANY)
    vmem = pl.BlockSpec(memory_space=pltpu.VMEM)
    wt = weight.T
    dma = pltpu.SemaphoreType.DMA
    chunk_rows = [2 * nv for _, nv in VCHUNKS]
    spec, wg = pl.pallas_call(
        functools.partial(first_kernel, nlat),
        out_shape=[
            pltpu.VMEM((1, ORDERS_PER, DEGREES, 2, CH), BF16),
            pltpu.VMEM((NVAR, CH), F32),
        ],
        in_specs=[any_spec] * 3 + [vmem] * 2 + [any_spec] * 2 + [vmem] + [any_spec],
        out_specs=[vmem, vmem],
        scratch_shapes=[
            pltpu.VMEM((ROWS, NLON, CH), BF16),
            pltpu.VMEM((NVAR, ROWS, NLON), BF16),
            pltpu.VMEM((NVAR, ROWS, NLON), BF16),
            pltpu.VMEM((nlat * MPAD, LPAD), BF16),
            pltpu.VMEM((8, 128), F32),
            pltpu.VMEM((16, npts), F32),
            pltpu.VMEM((NTILE, 4 * NVAR, 128), F32),
            pltpu.VMEM((NTILE, 4 * NVAR, 128), F32),
            pltpu.VMEM((4 * NVAR, LPAD), F32),
            pltpu.VMEM((4 * NVAR, LPAD), BF16),
        ]
        + [pltpu.VMEM((ENS, n, LBLK), BF16) for n in chunk_rows] * 2
        + [
            pltpu.VMEM((4 * NVAR, LPAD), BF16),
            pltpu.VMEM((nlat, MPAD, 128), BF16),
            pltpu.VMEM((nlat, MPAD, 128), BF16),
            pltpu.VMEM((nlat, 8, 128), BF16),
            pltpu.VMEM((nlat, MPAD, 128), BF16),
            pltpu.VMEM((nlat, MPAD, 128), BF16),
            pltpu.VMEM((nlat, 8, 128), BF16),
            pltpu.VMEM((nlat * MPAD, 128), F32),
            pltpu.VMEM((nlat * 8, 128), F32),
            pltpu.VMEM((2 * NVAR, LBLK), F32),
            pltpu.VMEM((2 * NVAR, 128), F32),
            pltpu.VMEM((NVAR, CH), F32),
            pltpu.VMEM((2, 8, CH), F32),
            pltpu.VMEM((2 * ENS, 8, CH), F32),
            pltpu.VMEM((2 * nz, 8, CH), F32),
            pltpu.VMEM((OCTETS, 8, CH), F32),
            pltpu.VMEM((DEGREES * 16, npts), F32),
            pltpu.VMEM((2, 2 * DEGREES, npts), F32),
            pltpu.VMEM((ORDERS_PER, 2 * DEGREES, 2 * npts), BF16),
            pltpu.VMEM((2, nlat * MPAD, 128), F32),
            pltpu.VMEM((nlat * 8, 128), F32),
            pltpu.VMEM((128, ROWS * CH), BF16),
            pltpu.VMEM((256, ROWS * CH), BF16),
            pltpu.VMEM((128, ROWS * CH), F32),
            pltpu.VMEM((nlat * MP, 128), BF16),
            pltpu.VMEM((nlat * MP, 256), BF16),
            pltpu.VMEM((nlat * MP, ROWS * CH), F32),
            pltpu.VMEM((ORDERS_PER, 2 * npts, CH), BF16),
            dma((9,)), dma((3,)), dma((3,)), dma((3,)), dma((3,)), dma((3,)), dma((3,)),
            dma((OCTETS + 2,)), dma((2,)), dma,
        ],
        compiler_params=pltpu.CompilerParams(
            collective_id=0, has_side_effects=True, vmem_limit_bytes=60 * 1024 * 1024
        ),
        name="loss_and_transform",
    )(features, previous, target, wt, var_weight.reshape(1, NVAR),
      jnp.asarray(basis), jnp.asarray(area), jnp.asarray(cosine), jnp.asarray(diag))

    return spec, wg.T


def solution(mesh):
    placed = (
        P("ens", "lat", None, None),
        P("ens", None, "lat", None),
        P(None, "lat", None),
        P(),
        P(),
    )
    return jax.shard_map(
        functools.partial(local, mesh.shape["lat"]),
        mesh=mesh,
        in_specs=placed,
        out_specs=(P("ens", "lat", None, None, None), P()),
        check_vma=False,
    )
```
